32 devices in a mesh: env: 4 (over x, core), tm: 8 (over z, y).
Axes of the slice: x: 2, y: 2, z: 4, core: 2. Of those that a mesh axis runs over, the one named last changes fastest.
Arguments:
- hidden: bfloat16 [4, 8, 256, 1024], P('env', 'tm'), may hold values from -6 to 6
- done_step: int32 [4, 8], P('env', 'tm'), may hold values from 0 to 255
- alive: int32 [4, 8, 256], P('env', None, 'tm'), may hold values 0 or 1
- targets: float32 [4, 8, 256], P('env', None, 'tm'), may hold values from -6 to 6
- gain_t: float32 [1024], replicated, may hold values from 0.25 to 1.75
- w_qkv_t: bfloat16 [1024, 3072], replicated, may hold values from -5 to 5
- w_out_t: bfloat16 [1024, 1024], replicated, may hold values from -0.1875 to 0.1875
- gain_a: float32 [1024], replicated, may hold values from 0.25 to 1.75
- w_qkv_a: bfloat16 [1024, 3072], P('tm'), may hold values from -5 to 5
- w_out_a: bfloat16 [1024, 1024], P('tm'), may hold values from -0.1875 to 0.1875
- w_value: float32 [1024], replicated, may hold values from -0.1875 to 0.1875
Outputs:
- values: float32 [4, 8, 256], P('env', None, 'tm')
- input_grad: bfloat16 [4, 8, 256, 1024], P('env', 'tm')
- qkv_grad: float32 [1024, 3072], P('tm')
- out_grad: float32 [1024, 1024], P('tm')
The draws below stay inside these ranges and needn't reach their ends.
Inputs may be any that keep to these rules, and one draw needn't show every extreme that they name: `done_step`: the last step of an agent's first episode in the window; later steps form a new episode.
All inputs are finite; a program needn't handle non-finite values. No bound on the sum of `alive` on one device may be relied on, other than what follows from the above.
Results may differ from the reference program's by a relative error of at most 0.02.
Values may be sent and summed in bfloat16 or wider, within the bound.
No kernel may reach another device: no remote copies, remote signals or barrier semaphores. Data moves between devices by JAX's collectives and lax.ppermute only.
A program may use at most 128 MiB of HBM per device.

```python
import math
import jax
import jax.numpy as jnp
from jax import lax

D = 1024
HEADS = 8
STEPS = 256
AGENTS = 8
ENVS = 4


def projection_draw(key):
    base = jax.random.normal(key, (D, 3 * D), jnp.float32) / math.sqrt(D)
    return jnp.clip(base, -5.0, 5.0)


def draw_w_qkv_t(key, part):
    return projection_draw(jax.random.fold_in(key, 11)).astype(jnp.bfloat16)


def draw_w_qkv_a(key, part):
    return projection_draw(jax.random.fold_in(key, 23)).astype(jnp.bfloat16)


def set_ends(result, stream_key, smallest, largest):
    spot = [jax.random.randint(jax.random.fold_in(stream_key, axis), (), 0, length) for axis, length in enumerate(result.shape)]
    main_axis = result.shape.index(max(result.shape))
    neighbour = spot[:main_axis] + [(spot[main_axis] + 1) % result.shape[main_axis]] + spot[main_axis + 1:]
    return result.at[tuple(spot)].set(smallest).at[tuple(neighbour)].set(largest)


def block_scale(own_key, shape, shards, low, high):
    factor_of, own = 1.0, jax.random.fold_in(own_key, 6)
    for axis_at, parts in shards:
        heights = jnp.exp(jax.random.uniform(jax.random.fold_in(own, axis_at), (parts,), jnp.float32, low / len(shards), high / len(shards)))
        factor_of = factor_of * jnp.repeat(heights, shape[axis_at] // parts).reshape([-1 if axis == axis_at else 1 for axis in range(len(shape))])
    return factor_of


def normal_values(stream_key, shape, spread, most, shards=(), held_as=jnp.bfloat16):
    drawn = spread * jax.random.normal(stream_key, shape, jnp.float32)
    if shards:
        drawn = drawn * block_scale(stream_key, shape, shards, -0.22, 0.18)
    return jnp.clip(drawn, -most, most).astype(held_as)


def setup_inputs(seed: int = 0) -> dict:
    splits = jax.random.split(jax.random.key(seed), 12)
    hidden = normal_values(splits[0], (ENVS, AGENTS, STEPS, D), 1.0, 6.0, ((0, 4), (1, 8)))
    done_step = set_ends(jax.random.randint(splits[1], (ENVS, AGENTS), 0, STEPS), jax.random.fold_in(splits[1], 1), 0, STEPS - 1).astype(jnp.int32)
    alive = set_ends((jax.random.randint(splits[2], (ENVS, AGENTS, STEPS), 0, 4) < 3).astype(jnp.int32), jax.random.fold_in(splits[2], 1), 0, 1)
    targets = normal_values(splits[3], (ENVS, AGENTS, STEPS), 1.0, 6.0, ((0, 4), (2, 8)), jnp.float32)
    gain_t = jnp.clip(1.0 + 0.15 * jax.random.normal(splits[4], (D,), jnp.float32), 0.25, 1.75)
    w_qkv_t = draw_w_qkv_t(jax.random.fold_in(splits[11], 71), 0)
    w_out_t = normal_values(splits[6], (D, D), D ** -0.5, 0.1875)
    gain_a = jnp.clip(1.0 + 0.15 * jax.random.normal(splits[7], (D,), jnp.float32), 0.25, 1.75)
    w_qkv_a = draw_w_qkv_a(jax.random.fold_in(splits[11], 71), 0)
    w_out_a = normal_values(splits[9], (D, D), D ** -0.5, 0.1875, ((0, 8),))
    w_value = normal_values(splits[10], (D,), D ** -0.5, 0.1875, (), jnp.float32)
    return {"hidden": hidden, "done_step": done_step, "alive": alive, "targets": targets, "gain_t": gain_t, "w_qkv_t": w_qkv_t, "w_out_t": w_out_t, "gain_a": gain_a, "w_qkv_a": w_qkv_a, "w_out_a": w_out_a, "w_value": w_value}


def norm_scale(rows, gain):
    return rows * lax.rsqrt(lax.optimization_barrier(jnp.mean(rows * rows, axis=-1, keepdims=True)) + 1e-06) * gain

def attend(qkv, allowed, head_count, layout):
    width = qkv.shape[-1] // 3
    size = width // head_count
    shape = qkv.shape[:-1] + (head_count, size)
    queries = qkv[..., :width].reshape(shape).astype(jnp.float32)
    key_rows = qkv[..., width:2 * width].reshape(shape).astype(jnp.float32)
    value_rows = qkv[..., 2 * width:].reshape(shape).astype(jnp.float32)
    if layout == 'temporal':
        score_form = 'bqhe,bkhe->bhqk'
        mix_form = 'bhqk,bkhe->bqhe'
    else:
        score_form = 'qbhe,kbhe->bhqk'
        mix_form = 'bhqk,kbhe->qbhe'
    scores = jnp.einsum(score_form, queries, key_rows) / math.sqrt(size)
    scores = jnp.where(allowed[:, None], scores, -1e+30)
    row_max = lax.optimization_barrier(jnp.max(scores, axis=-1, keepdims=True))
    weights = jnp.exp(scores - row_max)
    probs = (weights / lax.optimization_barrier(jnp.sum(weights, axis=-1, keepdims=True))).astype(jnp.bfloat16)
    mixed = jnp.einsum(mix_form, probs.astype(jnp.float32), value_rows)
    return mixed.reshape(qkv.shape[:-1] + (width,))

def temporal_block(rows, done, gain, w_qkv, w_out, head_count):
    batch, length, width = rows.shape
    rows_f = rows.astype(jnp.float32)
    normed = norm_scale(rows_f, gain).astype(jnp.bfloat16)
    qkv = jnp.dot(normed.reshape(-1, width), w_qkv, preferred_element_type=jnp.float32)
    qkv = qkv.astype(jnp.bfloat16).reshape(batch, length, 3 * width)
    positions = jnp.arange(length, dtype=jnp.int32)
    later = positions[None, :] > done[:, None]
    causal = positions[:, None] >= positions[None, :]
    allowed = causal[None] & (later[:, :, None] == later[:, None, :])
    mixed = attend(qkv, allowed, head_count, 'temporal').astype(jnp.bfloat16)
    added = jnp.dot(mixed.reshape(-1, width), w_out, preferred_element_type=jnp.float32)
    return (rows_f + added.reshape(batch, length, width)).astype(jnp.bfloat16)

def left_product(left, right):
    return lax.dot_general(left, right, (((0,), (0,)), ((), ())), preferred_element_type=jnp.float32)

def agent_step(lifted, alive_rows, target_rows, gain, w_qkv, w_out, w_value, head_count):
    agent_count, step_count, width = lifted.shape
    lifted_f = lifted.astype(jnp.float32)
    normed_f, norm_pull = jax.vjp(lambda rows: norm_scale(rows, gain), lifted_f)
    normed = normed_f.astype(jnp.bfloat16).reshape(-1, width)
    qkv = jnp.dot(normed, w_qkv, preferred_element_type=jnp.float32)
    qkv = qkv.astype(jnp.bfloat16).reshape(agent_count, step_count, 3 * width)
    living = alive_rows.T == 1
    allowed = living[:, None, :] | jnp.eye(agent_count, dtype=bool)[None]
    mixed_f, attend_pull = jax.vjp(lambda block: attend(block, allowed, head_count, 'agents'), qkv)
    mixed = mixed_f.astype(jnp.bfloat16).reshape(-1, width)
    added = jnp.dot(mixed, w_out, preferred_element_type=jnp.float32)
    top_rows = lifted_f + added.reshape(agent_count, step_count, width)
    predicted = lax.optimization_barrier(jnp.sum(top_rows * w_value, axis=-1))
    residual_err = 32.0 * alive_rows.astype(jnp.float32) * (predicted - target_rows)
    grad_top = residual_err[..., None] * w_value
    grad_rows = grad_top.astype(jnp.bfloat16).reshape(-1, width)
    grad_mixed = jnp.dot(grad_rows, w_out.T, preferred_element_type=jnp.float32)
    grad_qkv = attend_pull(grad_mixed.reshape(agent_count, step_count, width))[0]
    grad_qkv = grad_qkv.reshape(-1, 3 * width)
    grad_normed = jnp.dot(grad_qkv, w_qkv.T, preferred_element_type=jnp.float32)
    grad_lifted = grad_top + norm_pull(grad_normed.reshape(agent_count, step_count, width))[0]
    return (predicted, grad_lifted.astype(jnp.bfloat16), normed, grad_qkv, mixed, grad_rows)

def reference(hidden, done_step, alive, targets, gain_t, w_qkv_t, w_out_t, gain_a, w_qkv_a, w_out_a, w_value):
    predicted_all = []
    input_all = []
    qkv_total = jnp.zeros((D, 3 * D), jnp.float32)
    out_total = jnp.zeros((D, D), jnp.float32)
    for env_index in range(ENVS):
        done_rows = done_step[env_index]
        first, pull = jax.vjp(lambda rows: temporal_block(rows, done_rows, gain_t, w_qkv_t, w_out_t, HEADS), hidden[env_index])
        lifted = jnp.swapaxes(first, 0, 1)
        lifted = jnp.swapaxes(lifted, 0, 1)
        predicted, grad_lifted, normed, grad_qkv, mixed, grad_rows = agent_step(lifted, alive[env_index], targets[env_index], gain_a, w_qkv_a, w_out_a, w_value, HEADS)
        qkv_total = qkv_total + left_product(normed, grad_qkv)
        out_total = out_total + left_product(mixed, grad_rows)
        input_all.append(pull(grad_lifted)[0])
        predicted_all.append(predicted)
    return (jnp.stack(predicted_all), jnp.stack(input_all), qkv_total, out_total)
```

```python
import functools
import math

import jax
import jax.numpy as jnp
from jax import lax
from jax.experimental import pallas as pl
from jax.experimental.pallas import tpu as pltpu
from jax.sharding import PartitionSpec as P

HEADS = 8
EPS = 1e-06
F32 = jnp.float32
BF16 = jnp.bfloat16
TILE = 256
VMEM_BYTES = 40 * 1024 * 1024


def dot_nn(a, b):
    return lax.dot_general(a, b, (((1,), (0,)), ((), ())), preferred_element_type=F32)


def dot_nt(a, b):
    return lax.dot_general(a, b, (((1,), (1,)), ((), ())), preferred_element_type=F32)


def dot_tn(a, b):
    return lax.dot_general(a, b, (((0,), (0,)), ((), ())), preferred_element_type=F32)


def inv_rms(rows):
    return lax.rsqrt(jnp.mean(rows * rows, axis=-1, keepdims=True) + EPS)


def norm_pull(rows, gain, grad):
    scale = inv_rms(rows)
    scaled = grad * gain
    inner = jnp.mean(scaled * rows, axis=-1, keepdims=True)
    return scale * scaled - rows * (scale * scale * scale * inner)


def spans(total, size):
    size = min(size, total)
    return [pl.ds(at, size) for at in range(0, total, size)]


def temporal_forward(
    done_ref, rows_ref, gain_ref, w_qkv_hbm, w_out_hbm, h1_ref, qkv_ref, probs_ref,
    w_qkv, w_out, mixed, sems,
):
    length, width = rows_ref.shape
    size = width // HEADS
    copies = []
    for part in range(3):
        span = pl.ds(part * width, width)
        copies.append(
            pltpu.make_async_copy(w_qkv_hbm.at[:, span], w_qkv.at[:, span], sems.at[part])
        )
    copies.append(pltpu.make_async_copy(w_out_hbm, w_out, sems.at[3]))
    for copy in copies:
        copy.start()
    rows = rows_ref[...].astype(F32)
    normed = (rows * inv_rms(rows) * gain_ref[...]).astype(BF16)
    for part in range(3):
        copies[part].wait()
        for at in range(part * width, (part + 1) * width, TILE):
            span = pl.ds(at, TILE)
            qkv_ref[:, span] = dot_nn(normed, w_qkv[:, span]).astype(BF16)
    done = done_ref[0]
    query_at = lax.broadcasted_iota(jnp.int32, (length, length), 0)
    key_at = lax.broadcasted_iota(jnp.int32, (length, length), 1)
    allowed = (key_at <= query_at) & ((key_at > done) == (query_at > done))
    bias = jnp.where(allowed, 0.0, -1e30)
    for head in range(HEADS):
        queries = qkv_ref[:, pl.ds(head * size, size)]
        keys = qkv_ref[:, pl.ds(width + head * size, size)]
        values = qkv_ref[:, pl.ds(2 * width + head * size, size)]
        scores = dot_nt(queries, keys) * (1.0 / math.sqrt(size)) + bias
        weights = jnp.exp(scores - jnp.max(scores, axis=-1, keepdims=True))
        probs = weights * (1.0 / jnp.sum(weights, axis=-1, keepdims=True))
        probs = probs.astype(BF16)
        probs_ref[head] = probs
        mixed[:, pl.ds(head * size, size)] = dot_nn(probs, values).astype(BF16)
    copies[3].wait()
    for span in spans(width, TILE):
        added = dot_nn(mixed[...], w_out[:, span])
        h1_ref[:, span] = (rows_ref[:, span].astype(F32) + added).astype(BF16)


def temporal_backward(
    grad_ref, rows_ref, gain_ref, qkv_ref, probs_ref, w_qkv_hbm, w_out_hbm, out_ref,
    w_qkv, w_out, grad_mixed, grad_qkv, grad_normed, sems,
):
    length, width = rows_ref.shape
    size = width // HEADS
    scale = 1.0 / math.sqrt(size)
    copies = [
        pltpu.make_async_copy(w_out_hbm, w_out, sems.at[0]),
        pltpu.make_async_copy(w_qkv_hbm, w_qkv, sems.at[1]),
    ]
    for copy in copies:
        copy.start()
    copies[0].wait()
    grad = grad_ref[...]
    for span in spans(width, TILE):
        grad_mixed[:, span] = dot_nt(grad, w_out[span, :]).astype(BF16)
    for head in range(HEADS):
        query_span = pl.ds(head * size, size)
        key_span = pl.ds(width + head * size, size)
        value_span = pl.ds(2 * width + head * size, size)
        probs = probs_ref[head]
        head_grad = grad_mixed[:, query_span]
        grad_qkv[:, value_span] = dot_tn(probs, head_grad).astype(BF16)
        grad_probs = dot_nt(head_grad, qkv_ref[:, value_span])
        wide = probs.astype(F32)
        inner = jnp.sum(wide * grad_probs, axis=-1, keepdims=True)
        grad_scores = (wide * (grad_probs - inner) * scale).astype(BF16)
        grad_qkv[:, query_span] = dot_nn(grad_scores, qkv_ref[:, key_span]).astype(BF16)
        grad_qkv[:, key_span] = dot_tn(grad_scores, qkv_ref[:, query_span]).astype(BF16)
    copies[1].wait()
    for span in spans(width, TILE):
        grad_normed[:, span] = dot_nt(grad_qkv[...], w_qkv[span, :])
    rows = rows_ref[...].astype(F32)
    pulled = norm_pull(rows, gain_ref[...], grad_normed[...])
    out_ref[...] = (grad_ref[...].astype(F32) + pulled).astype(BF16)


def agent_kernel(
    blocks, group_steps, place_ref, rows_ref, alive_ref, target_ref, gain_ref, value_ref,
    folded_ref, shard_hbm, *rest,
):
    moved = rest[: 2 * blocks]
    grad_ref, normed_ref, grad_qk_ref, folded_grad_ref, predicted_ref = rest[2 * blocks : 2 * blocks + 5]
    w_qk, qk, probs_all, slopes, column, grad_normed, sems = rest[2 * blocks + 5 :]
    total_rows, width = rows_ref.shape
    size = width // HEADS
    scale = 1.0 / math.sqrt(size)
    groups, group_rows = alive_ref.shape[0], alive_ref.shape[2]
    agents = group_rows // group_steps
    local_steps = total_rows // agents
    depth = shard_hbm.shape[0]

    copies = [
        pltpu.make_async_copy(
            shard_hbm.at[:, pl.ds(0, 2 * width)],
            w_qk.at[pl.ds(pl.multiple_of(place_ref[2 * blocks] * depth, depth), depth), :],
            sems.at[2 * blocks],
        )
    ]
    for at in range(2 * blocks):
        half = place_ref[2 * blocks + 1 + at // blocks]
        target = w_qk.at[
            pl.ds(pl.multiple_of(place_ref[at] * depth, depth), depth),
            pl.ds(pl.multiple_of(half * width, width), width),
        ]
        copies.append(pltpu.make_async_copy(moved[at], target, sems.at[at]))
    for copy in copies:
        copy.start()

    def row_spans(group):
        if groups == 1:
            return [(pl.ds(0, total_rows), pl.ds(0, total_rows))]
        return [
            (
                pl.ds(agent * local_steps + group * group_steps, group_steps),
                pl.ds(group * group_rows + agent * group_steps, group_steps),
            )
            for agent in range(agents)
        ]

    def to_column(row):
        return jnp.transpose(jnp.broadcast_to(row, (128, row.shape[1])))[:, :1]

    for group in range(groups):
        for source, target in row_spans(group):
            rows = rows_ref[source, :].astype(F32)
            normed_ref[target, :] = (rows * inv_rms(rows) * gain_ref[...]).astype(BF16)
            column[target, :] = jnp.broadcast_to(
                jnp.sum(rows * value_ref[...], axis=-1, keepdims=True), (rows.shape[0], 128)
            )
    both = dot_nt(folded_ref[...], normed_ref[...])
    folded_rows = both[:HEADS] + both[HEADS:]
    for copy in copies:
        copy.wait()
    for span in spans(2 * width, TILE):
        qk[:, span] = dot_nn(normed_ref[...], w_qk[:, span]).astype(BF16)

    row_at = lax.broadcasted_iota(jnp.int32, (group_rows, group_rows), 0)
    col_at = lax.broadcasted_iota(jnp.int32, (group_rows, group_rows), 1)
    same_step = row_at % group_steps == col_at % group_steps
    pulls = []
    for group in range(groups):
        group_span = pl.ds(group * group_rows, group_rows)
        alive = alive_ref[group]
        allowed = same_step & ((alive > 0.5) | (row_at == col_at))
        bias = jnp.where(allowed, 0.0, -1e30)
        predicted = column[group_span, :1]
        for head in range(HEADS):
            queries = qk[group_span, pl.ds(head * size, size)]
            keys = qk[group_span, pl.ds(width + head * size, size)]
            scores = dot_nt(queries, keys) * scale + bias
            weights = jnp.exp(scores - jnp.max(scores, axis=-1, keepdims=True))
            probs = weights * (1.0 / jnp.sum(weights, axis=-1, keepdims=True))
            weighted = probs * folded_rows[
                head : head + 1, group * group_rows : (group + 1) * group_rows
            ]
            pooled = jnp.sum(weighted, axis=-1, keepdims=True)
            predicted = predicted + pooled
            probs_all[group * HEADS + head] = probs
            slopes[group * HEADS + head] = (weighted - probs * pooled) * scale
        error = 32.0 * to_column(alive) * (predicted - to_column(target_ref[group]))
        predicted_ref[group] = jnp.transpose(jnp.broadcast_to(predicted, (group_rows, 128)))[:8]
        column[group_span, :] = jnp.broadcast_to(error, (group_rows, 128))
        pull_rows = []
        for head in range(HEADS):
            query_span = pl.ds(head * size, size)
            key_span = pl.ds(width + head * size, size)
            grad_scores = (slopes[group * HEADS + head] * error).astype(BF16)
            grad_qk_ref[group_span, query_span] = dot_nn(
                grad_scores, qk[group_span, key_span]
            ).astype(BF16)
            grad_qk_ref[group_span, key_span] = dot_tn(
                grad_scores, qk[group_span, query_span]
            ).astype(BF16)
            pull_rows.append(
                jnp.sum(probs_all[group * HEADS + head] * error, axis=0, keepdims=True)
            )
        pulls.append(jnp.concatenate(pull_rows, axis=0))
    pull = jnp.concatenate(pulls, axis=1) if groups > 1 else pulls[0]
    pull = pull.astype(BF16)
    twice = jnp.concatenate([pull, pull], axis=0)
    for span in spans(width, TILE):
        grad_normed[:, span] = dot_nt(grad_qk_ref[...], w_qk[span, :]) + dot_tn(
            twice, folded_ref[:, span]
        )
    for group in range(groups):
        for source, target in row_spans(group):
            rows = rows_ref[source, :].astype(F32)
            pulled = norm_pull(rows, gain_ref[...], grad_normed[target, :])
            top = column[target, :1] * value_ref[...]
            grad_ref[source, :] = (top + pulled).astype(BF16)
    folded_grad_ref[...] = dot_nn(pull, normed_ref[...])


def weight_grad_kernel(left_ref, right_ref, out_ref):
    for span in spans(out_ref.shape[1], TILE):
        out_ref[:, span] = dot_tn(left_ref[...], right_ref[:, span]).astype(BF16)


def any_spec():
    return pl.BlockSpec(memory_space=pl.ANY)


def vmem_spec():
    return pl.BlockSpec(memory_space=pltpu.VMEM)


def smem_spec():
    return pl.BlockSpec(memory_space=pltpu.SMEM)


def params():
    return pltpu.CompilerParams(vmem_limit_bytes=VMEM_BYTES)


def cost(flops, moved):
    return pl.CostEstimate(flops=flops, bytes_accessed=moved, transcendentals=0)


def ring_order(count):
    return list(range(0, count, 2)) + list(range(count - 1, 0, -2))


def per_device(
    env_count, tm_count,
    hidden, done_step, alive, targets, gain_t, w_qkv_t, w_out_t, gain_a, w_qkv_a, w_out_a, w_value,
):
    length, width = hidden.shape[2:]
    agents, local_steps = alive.shape[1:]
    depth = w_qkv_a.shape[0]
    size = width // HEADS
    env_at = lax.axis_index("env")
    tm_at = lax.axis_index("tm")
    core = env_at % 2
    order = ring_order(tm_count)
    spot = [order.index(at) for at in range(tm_count)]
    order_array = jnp.array(order, jnp.int32)
    my_spot = jnp.array(spot, jnp.int32)[tm_at]

    def ring(block, step):
        pairs = []
        for env in range(env_count):
            sign = 1 - 2 * (env % 2)
            for at in range(tm_count):
                pairs.append(
                    (env * tm_count + at, env * tm_count + order[(spot[at] + sign * step) % tm_count])
                )
        return lax.ppermute(block, ("env", "tm"), pairs)

    def swap_env(block, bit):
        return lax.ppermute(block, "env", [(at, at ^ bit) for at in range(env_count)])

    def sum_tm(block):
        bit = 1
        while bit < tm_count:
            block = block + lax.ppermute(block, "tm", [(at, at ^ bit) for at in range(tm_count)])
            bit *= 2
        return block

    def sum_env(block):
        bit = 1
        while bit < env_count:
            block = block + swap_env(block, bit)
            bit *= 2
        return block

    far = tm_count // 2
    near = tm_count - 1 - far
    own_half = lax.dynamic_slice(w_qkv_a, (0, core * width), (depth, width))
    forward, backward = [own_half], [own_half]
    for step in range(far):
        forward.append(ring(forward[-1], 1))
        if step < near:
            backward.append(ring(backward[-1], -1))
    own_blocks = forward[1:] + backward[1:]
    other_blocks = [swap_env(block, 1) for block in own_blocks]
    hops = jnp.array([-step for step in range(1, far + 1)] + list(range(1, near + 1)), jnp.int32)
    sign = 1 - 2 * core
    own_places = order_array[(my_spot + sign * hops) % tm_count]
    other_places = order_array[(my_spot - sign * hops) % tm_count]
    places = jnp.concatenate(
        [own_places, other_places, jnp.stack([tm_at, core, 1 - core])]
    ).astype(jnp.int32)

    rows = hidden[0, 0]
    h1, qkv, probs = pl.pallas_call(
        temporal_forward,
        name="temporal_forward",
        out_shape=(
            jax.ShapeDtypeStruct((length, width), BF16),
            jax.ShapeDtypeStruct((length, 3 * width), BF16),
            jax.ShapeDtypeStruct((HEADS, length, length), BF16),
        ),
        in_specs=[smem_spec(), vmem_spec(), vmem_spec(), any_spec(), any_spec()],
        out_specs=[vmem_spec()] * 3,
        scratch_shapes=[
            pltpu.VMEM((width, 3 * width), BF16),
            pltpu.VMEM((width, width), BF16),
            pltpu.VMEM((length, width), BF16),
            pltpu.SemaphoreType.DMA((4,)),
        ],
        compiler_params=params(),
        cost_estimate=cost(8 * length * width * width, 8 * width * width),
    )(done_step[0], rows, gain_t[None], w_qkv_t, w_out_t)
    lifted = lax.all_to_all(h1, "tm", split_axis=0, concat_axis=0, tiled=True)

    local_u = jnp.sum(w_out_a.astype(F32) * w_value, axis=1)
    u = sum_tm(lax.dynamic_update_slice(jnp.zeros((width,), F32), local_u, (tm_at * depth,)))
    w_v = w_qkv_a[:, 2 * width :].astype(F32).reshape(depth, HEADS, size)
    local_folded = jnp.sum(w_v * u.reshape(HEADS, size), axis=-1).T
    folded = sum_tm(
        lax.dynamic_update_slice(jnp.zeros((HEADS, width), F32), local_folded, (0, tm_at * depth))
    )
    folded_high = folded.astype(BF16)
    folded_low = (folded - folded_high.astype(F32)).astype(BF16)
    folded_parts = jnp.concatenate([folded_high, folded_low], axis=0)

    group_steps = 16 if local_steps % 16 == 0 else local_steps
    groups = local_steps // group_steps
    group_rows = agents * group_steps

    def grouped(block):
        block = block.reshape(agents, groups, group_steps)
        return jnp.swapaxes(block, 0, 1).reshape(groups, 1, group_rows)

    total_rows = agents * local_steps
    grad_lifted, normed, grad_qk, folded_grad, predicted = pl.pallas_call(
        functools.partial(agent_kernel, tm_count - 1, group_steps),
        name="agent_block",
        out_shape=(
            jax.ShapeDtypeStruct((total_rows, width), BF16),
            jax.ShapeDtypeStruct((total_rows, width), BF16),
            jax.ShapeDtypeStruct((total_rows, 2 * width), BF16),
            jax.ShapeDtypeStruct((HEADS, width), F32),
            jax.ShapeDtypeStruct((groups, 8, group_rows), F32),
        ),
        in_specs=[smem_spec()] + [vmem_spec()] * 6 + [any_spec()] * (2 * tm_count - 1),
        out_specs=[vmem_spec()] * 5,
        scratch_shapes=[
            pltpu.VMEM((width, 2 * width), BF16),
            pltpu.VMEM((total_rows, 2 * width), BF16),
            pltpu.VMEM((groups * HEADS, group_rows, group_rows), F32),
            pltpu.VMEM((groups * HEADS, group_rows, group_rows), F32),
            pltpu.VMEM((total_rows, 128), F32),
            pltpu.VMEM((total_rows, width), F32),
            pltpu.SemaphoreType.DMA((2 * tm_count - 1,)),
        ],
        compiler_params=params(),
        cost_estimate=cost(8 * total_rows * width * width, 4 * width * width),
    )(
        places, lifted, grouped(alive[0].astype(F32)), grouped(targets[0]), gain_a[None],
        w_value[None], folded_parts, w_qkv_a, *own_blocks, *other_blocks,
    )
    values = predicted[:, 0].reshape(groups, agents, group_steps)
    values = jnp.swapaxes(values, 0, 1).reshape(1, agents, local_steps)

    returned = lax.all_to_all(grad_lifted, "tm", split_axis=0, concat_axis=0, tiled=True)

    def weight_grad(half):
        columns = lax.dynamic_slice(grad_qk, (0, half * width), (total_rows, width))
        return pl.pallas_call(
            weight_grad_kernel,
            name="weight_grad",
            grid=(width // TILE,),
            out_shape=jax.ShapeDtypeStruct((width, width), BF16),
            in_specs=[
                pl.BlockSpec((total_rows, TILE), lambda at: (0, at)),
                pl.BlockSpec((total_rows, width), lambda at: (0, 0)),
            ],
            out_specs=pl.BlockSpec((TILE, width), lambda at: (at, 0)),
            compiler_params=params(),
            cost_estimate=cost(2 * total_rows * width * width, 3 * width * width),
        )(normed, columns)

    received = swap_env(weight_grad(1 - core), 1)
    kept = weight_grad(core)

    def term(hop):
        at = order_array[(my_spot + sign * hop) % tm_count] * depth
        return lax.dynamic_slice(kept, (at, 0), (depth, width)).astype(F32) + lax.dynamic_slice(
            received, (at, 0), (depth, width)
        ).astype(F32)

    ahead = term(far).astype(BF16)
    behind = term(-near).astype(BF16)
    for step in range(far):
        ahead = ring(ahead, 1)
        if step < far - 1:
            ahead = (term(far - 1 - step) + ahead.astype(F32)).astype(BF16)
        if step < near:
            behind = ring(behind, -1)
            if step < near - 1:
                behind = (term(-(near - 1 - step)) + behind.astype(F32)).astype(BF16)
    reduced = (term(0) + ahead.astype(F32) + behind.astype(F32)).astype(BF16)
    bit = 2
    while bit < env_count:
        reduced = (reduced.astype(F32) + swap_env(reduced, bit).astype(F32)).astype(BF16)
        bit *= 2
    other = swap_env(reduced, 1)
    first = jnp.where(core == 0, reduced, other)
    second = jnp.where(core == 0, other, reduced)

    folded_total = sum_tm(sum_env(folded_grad))
    own_folded = lax.dynamic_slice(folded_total, (0, tm_at * depth), (HEADS, depth))
    v_grad = (own_folded.T[:, :, None] * u.reshape(1, HEADS, size)).reshape(depth, width)
    pooled = sum_tm(jnp.sum(w_v * own_folded.T[:, :, None], axis=0).reshape(width))
    own_pooled = lax.dynamic_slice(pooled, (tm_at * depth,), (depth,))
    out_grad = own_pooled[:, None] * w_value[None, :]
    qkv_grad = jnp.concatenate([first.astype(F32), second.astype(F32), v_grad], axis=1)

    input_grad = pl.pallas_call(
        temporal_backward,
        name="temporal_backward",
        out_shape=jax.ShapeDtypeStruct((length, width), BF16),
        in_specs=[vmem_spec()] * 5 + [any_spec()] * 2,
        out_specs=vmem_spec(),
        scratch_shapes=[
            pltpu.VMEM((width, 3 * width), BF16),
            pltpu.VMEM((width, width), BF16),
            pltpu.VMEM((length, width), BF16),
            pltpu.VMEM((length, 3 * width), BF16),
            pltpu.VMEM((length, width), F32),
            pltpu.SemaphoreType.DMA((2,)),
        ],
        compiler_params=params(),
        cost_estimate=cost(8 * length * width * width, 8 * width * width),
    )(returned, rows, gain_t[None], qkv, probs, w_qkv_t, w_out_t)
    return values, input_grad[None, None], qkv_grad, out_grad


def solution(mesh):
    in_specs = (
        P("env", "tm", None, None),
        P("env", "tm"),
        P("env", None, "tm"),
        P("env", None, "tm"),
        P(),
        P(),
        P(),
        P(),
        P("tm", None),
        P("tm", None),
        P(),
    )
    out_specs = (P("env", None, "tm"), P("env", "tm", None, None), P("tm", None), P("tm", None))
    body = functools.partial(per_device, mesh.shape["env"], mesh.shape["tm"])
    return jax.shard_map(
        body, mesh=mesh, in_specs=in_specs, out_specs=out_specs, check_vma=False
    )
```

```python
import functools
import math

import jax
import jax.numpy as jnp
from jax import lax
from jax.experimental import pallas as pl
from jax.experimental.pallas import tpu as pltpu
from jax.sharding import PartitionSpec as P

HEADS = 8
EPS = 1e-06
F32 = jnp.float32
BF16 = jnp.bfloat16
TILE = 256


def dot_nn(a, b):
    return lax.dot_general(a, b, (((1,), (0,)), ((), ())), preferred_element_type=F32)


def dot_nt(a, b):
    return lax.dot_general(a, b, (((1,), (1,)), ((), ())), preferred_element_type=F32)


def dot_tn(a, b):
    return lax.dot_general(a, b, (((0,), (0,)), ((), ())), preferred_element_type=F32)


def inv_rms(rows):
    return lax.rsqrt(jnp.mean(rows * rows, axis=-1, keepdims=True) + EPS)


def norm_pull(rows, gain, grad):
    scale = inv_rms(rows)
    scaled = grad * gain
    inner = jnp.mean(scaled * rows, axis=-1, keepdims=True)
    return scale * scaled - rows * (scale * scale * scale * inner)


def spans(total, size):
    size = min(size, total)
    return [pl.ds(at, size) for at in range(0, total, size)]


def temporal_forward(
    done_ref, rows_ref, gain_ref, w_qkv_hbm, w_out_hbm, h1_ref, qkv_ref, probs_ref,
    w_qkv, w_out, mixed, sems,
):
    length, width = rows_ref.shape
    size = width // HEADS
    copies = []
    for part in range(3):
        span = pl.ds(part * width, width)
        copies.append(
            pltpu.make_async_copy(w_qkv_hbm.at[:, span], w_qkv.at[:, span], sems.at[part])
        )
    copies.append(pltpu.make_async_copy(w_out_hbm, w_out, sems.at[3]))
    for copy in copies:
        copy.start()
    rows = rows_ref[...].astype(F32)
    normed = (rows * inv_rms(rows) * gain_ref[...]).astype(BF16)
    for part in range(3):
        copies[part].wait()
        for at in range(part * width, (part + 1) * width, TILE):
            span = pl.ds(at, TILE)
            qkv_ref[:, span] = dot_nn(normed, w_qkv[:, span]).astype(BF16)
    done = done_ref[0]
    query_at = lax.broadcasted_iota(jnp.int32, (length, length), 0)
    key_at = lax.broadcasted_iota(jnp.int32, (length, length), 1)
    allowed = (key_at <= query_at) & ((key_at > done) == (query_at > done))
    bias = jnp.where(allowed, 0.0, -1e30)
    for head in range(HEADS):
        queries = qkv_ref[:, pl.ds(head * size, size)]
        keys = qkv_ref[:, pl.ds(width + head * size, size)]
        values = qkv_ref[:, pl.ds(2 * width + head * size, size)]
        scores = dot_nt(queries, keys) * (1.0 / math.sqrt(size)) + bias
        weights = jnp.exp(scores - jnp.max(scores, axis=-1, keepdims=True))
        probs = weights * (1.0 / jnp.sum(weights, axis=-1, keepdims=True))
        probs = probs.astype(BF16)
        probs_ref[head] = probs
        mixed[:, pl.ds(head * size, size)] = dot_nn(probs, values).astype(BF16)
    copies[3].wait()
    for span in spans(width, TILE):
        added = dot_nn(mixed[...], w_out[:, span])
        h1_ref[:, span] = (rows_ref[:, span].astype(F32) + added).astype(BF16)


def temporal_backward(
    grad_ref, rows_ref, gain_ref, qkv_ref, probs_ref, w_qkv, w_out, out_ref,
    grad_mixed, grad_qkv, grad_normed,
):
    length, width = rows_ref.shape
    size = width // HEADS
    scale = 1.0 / math.sqrt(size)
    grad = grad_ref[...]
    for span in spans(width, TILE):
        grad_mixed[:, span] = dot_nt(grad, w_out[span, :]).astype(BF16)
    for head in range(HEADS):
        query_span = pl.ds(head * size, size)
        key_span = pl.ds(width + head * size, size)
        value_span = pl.ds(2 * width + head * size, size)
        probs = probs_ref[head]
        head_grad = grad_mixed[:, query_span]
        grad_qkv[:, value_span] = dot_tn(probs, head_grad).astype(BF16)
        grad_probs = dot_nt(head_grad, qkv_ref[:, value_span])
        wide = probs.astype(F32)
        inner = jnp.sum(wide * grad_probs, axis=-1, keepdims=True)
        grad_scores = (wide * (grad_probs - inner) * scale).astype(BF16)
        grad_qkv[:, query_span] = dot_nn(grad_scores, qkv_ref[:, key_span]).astype(BF16)
        grad_qkv[:, key_span] = dot_tn(grad_scores, qkv_ref[:, query_span]).astype(BF16)
    for span in spans(width, TILE):
        grad_normed[:, span] = dot_nt(grad_qkv[...], w_qkv[span, :])
    rows = rows_ref[...].astype(F32)
    pulled = norm_pull(rows, gain_ref[...], grad_normed[...])
    out_ref[...] = (grad_ref[...].astype(F32) + pulled).astype(BF16)


def agent_kernel(
    blocks, group_steps, place_ref, rows_ref, alive_ref, target_ref, gain_ref, value_ref,
    shard_ref, own_ref, *rest,
):
    moved = rest[: 2 * blocks]
    grad_ref, pack_ref, keep_ref, extra_ref, u_ref, predicted_ref = rest[2 * blocks : 2 * blocks + 6]
    w_all, qk, grad_qk, probs_all, slopes, column, grad_normed, sems = rest[2 * blocks + 6 :]
    total_rows, width = rows_ref.shape
    size = width // HEADS
    scale = 1.0 / math.sqrt(size)
    normed_ref = pack_ref.at[pl.ds(0, total_rows), :]
    groups, group_rows = alive_ref.shape[0], alive_ref.shape[2]
    agents = group_rows // group_steps
    local_steps = total_rows // agents
    depth, block_width = own_ref.shape
    middle = width // 2
    w_q, w_k = w_all.at[:, pl.ds(0, width)], w_all.at[:, pl.ds(block_width, width)]
    w_v = [
        w_all.at[:, pl.ds(width, middle)],
        w_all.at[:, pl.ds(block_width + width, middle)],
    ]
    core, other = place_ref[2 * blocks + 1], place_ref[2 * blocks + 2]

    def row_span(at):
        return pl.ds(pl.multiple_of(place_ref[at] * depth, depth), depth)

    def column_span(start, length):
        return pl.ds(pl.multiple_of(start, 128), length)

    own_rows = row_span(2 * blocks)
    other_at = other * block_width
    moves = [
        (own_ref, w_all.at[own_rows, column_span(core * block_width, block_width)]),
        (
            own_ref.at[:, pl.ds(block_width - 128, 128)],
            w_all.at[own_rows, column_span(other_at + block_width - 128, 128)],
        ),
        (
            shard_ref.at[:, column_span(other * width, width)],
            w_all.at[own_rows, column_span(other_at, width)],
        ),
        (
            shard_ref.at[:, column_span(2 * width + other * middle, middle)],
            w_all.at[own_rows, column_span(other_at + width, middle)],
        ),
    ]
    for at in range(2 * blocks):
        half = core if at < blocks else other
        moves.append(
            (moved[at], w_all.at[row_span(at), column_span(half * block_width, block_width)])
        )
    copies = [
        pltpu.make_async_copy(source, target, sems.at[at])
        for at, (source, target) in enumerate(moves)
    ]
    for copy in copies:
        copy.start()

    def row_spans(group):
        if groups == 1:
            return [(pl.ds(0, total_rows), pl.ds(0, total_rows))]
        return [
            (
                pl.ds(agent * local_steps + group * group_steps, group_steps),
                pl.ds(group * group_rows + agent * group_steps, group_steps),
            )
            for agent in range(agents)
        ]

    def to_column(row):
        return jnp.transpose(jnp.broadcast_to(row, (128, row.shape[1])))[:, :1]

    for group in range(groups):
        for source, target in row_spans(group):
            rows = rows_ref[source, :].astype(F32)
            normed_ref[target, :] = (rows * inv_rms(rows) * gain_ref[...]).astype(BF16)
            column[target, :] = jnp.broadcast_to(
                jnp.sum(rows * value_ref[...], axis=-1, keepdims=True), (rows.shape[0], 128)
            )
    for copy in copies:
        copy.wait()

    u_parts = jnp.transpose(w_all[:, pl.ds(block_width - 128, 128)].astype(F32))
    u_high, u_low = u_parts[0:1], u_parts[1:2]
    u_ref[...] = u_high + u_low
    part_at = lax.broadcasted_iota(jnp.int32, (2 * HEADS, width), 0)
    head_at = lax.broadcasted_iota(jnp.int32, (2 * HEADS, width), 1) // size
    by_head = jnp.where(
        head_at == part_at % HEADS, jnp.where(part_at < HEADS, u_high, u_low), 0.0
    ).astype(BF16)
    both = dot_nt(by_head[:, :middle], w_v[0][...]) + dot_nt(by_head[:, middle:], w_v[1][...])
    folded = both[:HEADS] + both[HEADS:]
    folded_high = folded.astype(BF16)
    folded_parts = jnp.concatenate(
        [folded_high.astype(F32), folded - folded_high.astype(F32)], axis=0
    ).astype(BF16)
    both = dot_nt(folded_parts, normed_ref[...])
    folded_rows = both[:HEADS] + both[HEADS:]
    for at in range(0, width, TILE):
        qk[:, pl.ds(at, TILE)] = dot_nn(normed_ref[...], w_q[:, pl.ds(at, TILE)]).astype(BF16)
    for at in range(0, width, TILE):
        qk[:, pl.ds(width + at, TILE)] = dot_nn(
            normed_ref[...], w_k[:, pl.ds(at, TILE)]
        ).astype(BF16)

    row_at = lax.broadcasted_iota(jnp.int32, (group_rows, group_rows), 0)
    col_at = lax.broadcasted_iota(jnp.int32, (group_rows, group_rows), 1)
    same_step = row_at % group_steps == col_at % group_steps
    pulls = []
    for group in range(groups):
        group_span = pl.ds(group * group_rows, group_rows)
        alive = alive_ref[group]
        allowed = same_step & ((alive > 0.5) | (row_at == col_at))
        bias = jnp.where(allowed, 0.0, -1e30)
        predicted = column[group_span, :1]
        for head in range(HEADS):
            queries = qk[group_span, pl.ds(head * size, size)]
            keys = qk[group_span, pl.ds(width + head * size, size)]
            scores = dot_nt(queries, keys) * scale + bias
            weights = jnp.exp(scores - jnp.max(scores, axis=-1, keepdims=True))
            probs = weights * (1.0 / jnp.sum(weights, axis=-1, keepdims=True))
            weighted = probs * folded_rows[
                head : head + 1, group * group_rows : (group + 1) * group_rows
            ]
            pooled = jnp.sum(weighted, axis=-1, keepdims=True)
            predicted = predicted + pooled
            probs_all[group * HEADS + head] = probs
            slopes[group * HEADS + head] = (weighted - probs * pooled) * scale
        error = 32.0 * to_column(alive) * (predicted - to_column(target_ref[group]))
        predicted_ref[group] = jnp.transpose(jnp.broadcast_to(predicted, (group_rows, 128)))[:8]
        column[group_span, :] = jnp.broadcast_to(error, (group_rows, 128))
        pull_rows = []
        for head in range(HEADS):
            query_span = pl.ds(head * size, size)
            key_span = pl.ds(width + head * size, size)
            grad_scores = (slopes[group * HEADS + head] * error).astype(BF16)
            grad_qk[group_span, query_span] = dot_nn(
                grad_scores, qk[group_span, key_span]
            ).astype(BF16)
            grad_qk[group_span, key_span] = dot_tn(
                grad_scores, qk[group_span, query_span]
            ).astype(BF16)
            pull_rows.append(
                jnp.sum(probs_all[group * HEADS + head] * error, axis=0, keepdims=True)
            )
        pulls.append(jnp.concatenate(pull_rows, axis=0))
    pull = jnp.concatenate(pulls, axis=1) if groups > 1 else pulls[0]
    pull = pull.astype(BF16)
    twice = jnp.concatenate([pull, pull], axis=0)
    for at in range(0, width, TILE):
        span = pl.ds(at, TILE)
        grad_normed[:, span] = (
            dot_nt(grad_qk[:, pl.ds(0, width)], w_q[span, :])
            + dot_nt(grad_qk[:, pl.ds(width, width)], w_k[span, :])
            + dot_tn(twice, folded_parts[:, at : at + TILE])
        )
    for group in range(groups):
        for source, target in row_spans(group):
            rows = rows_ref[source, :].astype(F32)
            pulled = norm_pull(rows, gain_ref[...], grad_normed[target, :])
            top = column[target, :1] * value_ref[...]
            grad_ref[source, :] = (top + pulled).astype(BF16)
    keep_ref[...] = grad_qk[:, column_span(core * width, width)]
    pack_ref[pl.ds(total_rows, total_rows), :] = grad_qk[:, column_span(other * width, width)]

    folded_grad = dot_nn(pull, normed_ref[...])
    folded_grad_low = folded_grad.astype(BF16)
    pooled = jnp.concatenate(
        [dot_nn(folded_grad_low, w_v[0][...]), dot_nn(folded_grad_low, w_v[1][...])], axis=1
    )
    pooled = jnp.sum(
        jnp.where(head_at[:HEADS] == part_at[:HEADS], pooled, 0.0), axis=0, keepdims=True
    )
    extra = jnp.concatenate(
        [folded_grad, pooled, jnp.zeros((127 - HEADS, width), F32)], axis=0
    )
    extra_ref[...] = jnp.transpose(extra).astype(BF16)


def weight_grad_kernel(place_ref, pack_ref, keep_ref, moved_ref, extra_ref, *rest):
    outs, (total, sems) = rest[:-2], rest[-2:]
    half, width = keep_ref.shape
    depth = width // len(outs)
    own, other = pl.ds(0, half), pl.ds(half, half)
    total[:, pl.ds(width, 128)] = extra_ref[...]
    for rows in spans(width, TILE):
        for columns in spans(width, TILE):
            total[rows, columns] = (
                dot_tn(pack_ref[own, rows], keep_ref[:, columns])
                + dot_tn(moved_ref[own, rows], moved_ref[other, columns])
            ).astype(BF16)
    copies = [
        pltpu.make_async_copy(
            total.at[pl.ds(pl.multiple_of(place_ref[at] * depth, depth), depth), :],
            out,
            sems.at[at],
        )
        for at, out in enumerate(outs)
    ]
    for copy in copies:
        copy.start()
    for copy in copies:
        copy.wait()


def pack_block_kernel(core_ref, qk_ref, v_ref, w_out_ref, value_ref, out_ref):
    width, middle = qk_ref.shape[1], v_ref.shape[1]
    out_ref[:, pl.ds(0, width)] = qk_ref[...]
    out_ref[:, pl.ds(width, middle)] = v_ref[...]
    u = jnp.sum(w_out_ref[...].astype(F32) * value_ref[...], axis=-1, keepdims=True)
    high = u.astype(BF16).astype(F32)
    lane = lax.broadcasted_iota(jnp.int32, (qk_ref.shape[0], 128), 1)
    parts = jnp.where(lane == 0, high, jnp.where(lane == 1, u - high, 0.0))
    out_ref[:, pl.ds(width + middle, 128)] = parts.astype(BF16)


def finish_kernel(core_ref, own_ref, other_ref, u_ref, value_ref, qkv_ref, out_ref):
    width = u_ref.shape[1]
    size = width // HEADS
    own, other = own_ref[:, pl.ds(0, width)], other_ref[:, pl.ds(0, width)]
    core = core_ref[0]
    qkv_ref[:, pl.ds(pl.multiple_of(core * width, width), width)] = own.astype(F32)
    qkv_ref[:, pl.ds(pl.multiple_of((1 - core) * width, width), width)] = other.astype(F32)
    extra = own_ref[:, pl.ds(width, 128)].astype(F32) + other_ref[:, pl.ds(width, 128)].astype(F32)
    for head in range(HEADS):
        qkv_ref[:, pl.ds(2 * width + head * size, size)] = (
            extra[:, head : head + 1] * u_ref[:, pl.ds(head * size, size)]
        )
    out_ref[...] = extra[:, HEADS : HEADS + 1] * value_ref[...]


def any_spec():
    return pl.BlockSpec(memory_space=pl.ANY)


def hbm_spec():
    return pl.BlockSpec(memory_space=pltpu.HBM)


def vmem_spec():
    return pl.BlockSpec(memory_space=pltpu.VMEM)


def smem_spec():
    return pl.BlockSpec(memory_space=pltpu.SMEM)


def params(mebibytes):
    return pltpu.CompilerParams(vmem_limit_bytes=mebibytes * 1024 * 1024)


def cost(flops, moved):
    return pl.CostEstimate(flops=flops, bytes_accessed=moved, transcendentals=0)


def ring_order(count):
    return list(range(0, count, 2)) + list(range(count - 1, 0, -2))


def per_device(
    env_count, tm_count,
    hidden, done_step, alive, targets, gain_t, w_qkv_t, w_out_t, gain_a, w_qkv_a, w_out_a, w_value,
):
    length, width = hidden.shape[2:]
    agents, local_steps = alive.shape[1:]
    depth = w_qkv_a.shape[0]
    size = width // HEADS
    env_at = lax.axis_index("env")
    tm_at = lax.axis_index("tm")
    core = env_at % 2
    order = ring_order(tm_count)
    spot = [order.index(at) for at in range(tm_count)]
    order_array = jnp.array(order, jnp.int32)
    my_spot = jnp.array(spot, jnp.int32)[tm_at]

    ways = [1 if at in (0, 3) else -1 for at in range(env_count)]
    way = jnp.array(ways, jnp.int32)[env_at]

    def ring(block):
        pairs = [
            (env * tm_count + at, env * tm_count + order[(spot[at] + ways[env]) % tm_count])
            for env in range(env_count)
            for at in range(tm_count)
        ]
        return lax.ppermute(block, ("env", "tm"), pairs)

    def swap_core(block):
        return lax.ppermute(block, "env", [(at, at ^ 1) for at in range(env_count)])

    def swap_chip(block):
        return lax.ppermute(block, "env", [(at, at ^ 2) for at in range(env_count)])

    far = tm_count // 2
    near = tm_count - 1 - far

    def places(hops):
        return order_array[(my_spot + way * jnp.array(hops, jnp.int32)) % tm_count]

    core_index = core[None].astype(jnp.int32)
    block_width = width + width // 2 + 128
    own_block = pl.pallas_call(
        pack_block_kernel,
        name="pack_block",
        out_shape=jax.ShapeDtypeStruct((depth, block_width), BF16),
        grid_spec=pltpu.PrefetchScalarGridSpec(
            num_scalar_prefetch=1,
            grid=(1,),
            in_specs=[
                pl.BlockSpec((depth, width), lambda at, core: (0, core[0])),
                pl.BlockSpec((depth, width // 2), lambda at, core: (0, 4 + core[0])),
                pl.BlockSpec((depth, width), lambda at, core: (0, 0)),
                pl.BlockSpec((1, width), lambda at, core: (0, 0)),
            ],
            out_specs=pl.BlockSpec((depth, block_width), lambda at, core: (0, 0)),
        ),
        compiler_params=params(16),
        cost_estimate=cost(2 * depth * width, 8 * depth * width),
    )(core_index, w_qkv_a, w_qkv_a, w_out_a, w_value[None])
    first_block = ring(own_block)

    rows = hidden[0, 0]
    h1, qkv, probs = pl.pallas_call(
        temporal_forward,
        name="temporal_forward",
        out_shape=(
            jax.ShapeDtypeStruct((length, width), BF16),
            jax.ShapeDtypeStruct((length, 3 * width), BF16),
            jax.ShapeDtypeStruct((HEADS, length, length), BF16),
        ),
        in_specs=[smem_spec(), vmem_spec(), vmem_spec(), hbm_spec(), hbm_spec()],
        out_specs=[vmem_spec()] * 3,
        scratch_shapes=[
            pltpu.VMEM((width, 3 * width), BF16),
            pltpu.VMEM((width, width), BF16),
            pltpu.VMEM((length, width), BF16),
            pltpu.SemaphoreType.DMA((4,)),
        ],
        compiler_params=params(24),
        cost_estimate=cost(8 * length * width * width, 8 * width * width),
    )(done_step[0], rows, gain_t[None], w_qkv_t, w_out_t)
    h1, first_block = lax.optimization_barrier((h1, first_block))
    lifted = lax.all_to_all(h1, "tm", split_axis=0, concat_axis=0, tiled=True)

    ringed, crossed = [first_block], []
    for hop in range(1, far):
        if hop <= near:
            crossed.append(swap_chip(ringed[-1]))
        ringed.append(ring(ringed[-1]))
    crossed += [swap_chip(block) for block in ringed[len(crossed) : near]]
    own_blocks = ringed + crossed
    other_blocks = [swap_core(block) for block in own_blocks]
    ahead_hops = list(range(1, far + 1))
    behind_hops = list(range(1, near + 1))
    block_places = jnp.concatenate(
        [
            places([-hop for hop in ahead_hops] + behind_hops),
            places(ahead_hops + [-hop for hop in behind_hops]),
            jnp.stack([tm_at, core, 1 - core]).astype(jnp.int32),
        ]
    )

    group_steps = 16 if local_steps % 16 == 0 else local_steps
    groups = local_steps // group_steps
    group_rows = agents * group_steps

    def grouped(block):
        block = block.reshape(agents, groups, group_steps)
        return jnp.swapaxes(block, 0, 1).reshape(groups, 1, group_rows)

    total_rows = agents * local_steps
    grad_lifted, pack, keep, extra, u, predicted = pl.pallas_call(
        functools.partial(agent_kernel, tm_count - 1, group_steps),
        name="agent_block",
        out_shape=(
            jax.ShapeDtypeStruct((total_rows, width), BF16),
            jax.ShapeDtypeStruct((2 * total_rows, width), BF16),
            jax.ShapeDtypeStruct((total_rows, width), BF16),
            jax.ShapeDtypeStruct((width, 128), BF16),
            jax.ShapeDtypeStruct((1, width), F32),
            jax.ShapeDtypeStruct((groups, 8, group_rows), F32),
        ),
        in_specs=[smem_spec()] + [vmem_spec()] * (2 * tm_count + 5),
        out_specs=[vmem_spec()] * 6,
        scratch_shapes=[
            pltpu.VMEM((width, 2 * block_width), BF16),
            pltpu.VMEM((total_rows, 2 * width), BF16),
            pltpu.VMEM((total_rows, 2 * width), BF16),
            pltpu.VMEM((groups * HEADS, group_rows, group_rows), F32),
            pltpu.VMEM((groups * HEADS, group_rows, group_rows), F32),
            pltpu.VMEM((total_rows, 128), F32),
            pltpu.VMEM((total_rows, width), F32),
            pltpu.SemaphoreType.DMA((2 * tm_count + 2,)),
        ],
        compiler_params=params(36),
        cost_estimate=cost(8 * total_rows * width * width, 4 * width * width),
    )(
        block_places, lifted, grouped(alive[0].astype(F32)), grouped(targets[0]), gain_a[None],
        w_value[None], w_qkv_a, own_block, *own_blocks, *other_blocks,
    )
    values = predicted[:, 0].reshape(groups, agents, group_steps)
    values = jnp.swapaxes(values, 0, 1).reshape(1, agents, local_steps)

    returned = lax.all_to_all(grad_lifted, "tm", split_axis=0, concat_axis=0, tiled=True)

    moved = swap_core(pack)
    hops = [0] + ahead_hops + [-hop for hop in behind_hops]
    terms = pl.pallas_call(
        weight_grad_kernel,
        name="weight_grad",
        out_shape=[jax.ShapeDtypeStruct((depth, width + 128), BF16)] * tm_count,
        in_specs=[smem_spec()] + [vmem_spec()] * 4,
        out_specs=[any_spec()] * tm_count,
        scratch_shapes=[
            pltpu.VMEM((width, width + 128), BF16),
            pltpu.SemaphoreType.DMA((tm_count,)),
        ],
        compiler_params=params(20),
        cost_estimate=cost(4 * total_rows * width * width, 4 * width * width),
    )(places(hops), pack, keep, moved, extra)
    term = dict(zip(hops, terms))
    chip_terms = {hop: swap_chip(term[-hop]) for hop in reversed(behind_hops)}
    travelling = ring(term[far])
    for hop in range(far - 1, 0, -1):
        travelling = travelling.astype(F32) + term[hop].astype(F32)
        if hop in chip_terms:
            travelling = travelling + chip_terms[hop].astype(F32)
        travelling = ring(travelling.astype(BF16))
    reduced = (travelling.astype(F32) + term[0].astype(F32)).astype(BF16)
    reduced = (reduced.astype(F32) + swap_chip(reduced).astype(F32)).astype(BF16)
    other = swap_core(reduced)
    qkv_grad, out_grad = pl.pallas_call(
        finish_kernel,
        name="finish",
        out_shape=(
            jax.ShapeDtypeStruct((depth, 3 * width), F32),
            jax.ShapeDtypeStruct((depth, width), F32),
        ),
        in_specs=[smem_spec()] + [vmem_spec()] * 4,
        out_specs=[vmem_spec()] * 2,
        compiler_params=params(16),
        cost_estimate=cost(8 * depth * width, 20 * depth * width),
    )(core_index, reduced, other, u, w_value[None])

    input_grad = pl.pallas_call(
        temporal_backward,
        name="temporal_backward",
        out_shape=jax.ShapeDtypeStruct((length, width), BF16),
        in_specs=[vmem_spec()] * 7,
        out_specs=vmem_spec(),
        scratch_shapes=[
            pltpu.VMEM((length, width), BF16),
            pltpu.VMEM((length, 3 * width), BF16),
            pltpu.VMEM((length, width), F32),
        ],
        compiler_params=params(30),
        cost_estimate=cost(8 * length * width * width, 8 * width * width),
    )(returned, rows, gain_t[None], qkv, probs, w_qkv_t, w_out_t)
    return values, input_grad[None, None], qkv_grad, out_grad


def solution(mesh):
    in_specs = (
        P("env", "tm", None, None),
        P("env", "tm"),
        P("env", None, "tm"),
        P("env", None, "tm"),
        P(),
        P(),
        P(),
        P(),
        P("tm", None),
        P("tm", None),
        P(),
    )
    out_specs = (P("env", None, "tm"), P("env", "tm", None, None), P("tm", None), P("tm", None))
    body = functools.partial(per_device, mesh.shape["env"], mesh.shape["tm"])
    return jax.shard_map(
        body, mesh=mesh, in_specs=in_specs, out_specs=out_specs, check_vma=False
    )
```

```python
import functools
import math

import jax
import jax.numpy as jnp
from jax import lax
from jax.experimental import pallas as pl
from jax.experimental.pallas import tpu as pltpu
from jax.sharding import PartitionSpec as P

HEADS = 8
EPS = 1e-06
F32 = jnp.float32
BF16 = jnp.bfloat16
TILE = 256
VMEM_BYTES = 60 * 1024 * 1024


def dot_nn(a, b):
    return lax.dot_general(a, b, (((1,), (0,)), ((), ())), preferred_element_type=F32)


def dot_nt(a, b):
    return lax.dot_general(a, b, (((1,), (1,)), ((), ())), preferred_element_type=F32)


def dot_tn(a, b):
    return lax.dot_general(a, b, (((0,), (0,)), ((), ())), preferred_element_type=F32)


def inv_rms(rows):
    return lax.rsqrt(jnp.mean(rows * rows, axis=-1, keepdims=True) + EPS)


def norm_pull(rows, gain, grad):
    scale = inv_rms(rows)
    scaled = grad * gain
    inner = jnp.mean(scaled * rows, axis=-1, keepdims=True)
    return scale * scaled - rows * (scale * scale * scale * inner)


def spans(total, size):
    size = min(size, total)
    return [pl.ds(at, size) for at in range(0, total, size)]


def core_of(env_ref):
    return env_ref[0] % 2


def place_of(env_ref, tm_ref, count, hop):
    at = tm_ref[0]
    way = 1 - 2 * ((env_ref[0] + env_ref[0] // 2) % 2)
    spot = jnp.where(at % 2 == 0, at // 2, count - 1 - at // 2)
    spot = (spot + way * hop + count) % count
    return jnp.where(spot < count // 2, 2 * spot, 2 * (count - 1 - spot) + 1)


def copies_of(moves, sems):
    return [
        pltpu.make_async_copy(source, target, sems.at[at])
        for at, (source, target) in enumerate(moves)
    ]


def started(moves, sems):
    copies = copies_of(moves, sems)
    for copy in copies:
        copy.start()
    return copies


def temporal_forward(
    done_ref, rows_ref, gain_ref, w_qkv_hbm, w_out_hbm, h1_ref, qkv_hbm, probs_hbm,
    w_qkv, w_out, qkv_ref, probs_ref, mixed, sems, out_sems,
):
    length, width = rows_ref.shape
    size = width // HEADS
    chunks = spans(3 * width, width // 2)
    moves = [(w_qkv_hbm.at[:, span], w_qkv.at[:, span]) for span in chunks]
    copies = started(moves + [(w_out_hbm, w_out)], sems)
    rows = rows_ref[...].astype(F32)
    normed = (rows * inv_rms(rows) * gain_ref[...]).astype(BF16)
    outs = copies_of(
        [(qkv_ref, qkv_hbm)] + [(probs_ref.at[head], probs_hbm.at[head]) for head in range(HEADS)],
        out_sems,
    )
    for part, chunk in enumerate(chunks):
        copies[part].wait()
        for at in range(chunk.start, chunk.start + chunk.size, TILE):
            span = pl.ds(at, TILE)
            qkv_ref[:, span] = dot_nn(normed, w_qkv[:, span]).astype(BF16)
    outs[0].start()
    done = done_ref[0]
    query_at = lax.broadcasted_iota(jnp.int32, (length, length), 0)
    key_at = lax.broadcasted_iota(jnp.int32, (length, length), 1)
    allowed = (key_at <= query_at) & ((key_at > done) == (query_at > done))
    bias = jnp.where(allowed, 0.0, -1e30)
    for head in range(HEADS):
        queries = qkv_ref[:, pl.ds(head * size, size)]
        keys = qkv_ref[:, pl.ds(width + head * size, size)]
        values = qkv_ref[:, pl.ds(2 * width + head * size, size)]
        scores = dot_nt(queries, keys) * (1.0 / math.sqrt(size)) + bias
        weights = jnp.exp(scores - jnp.max(scores, axis=-1, keepdims=True))
        probs = weights * (1.0 / jnp.sum(weights, axis=-1, keepdims=True))
        probs = probs.astype(BF16)
        probs_ref[head] = probs
        outs[1 + head].start()
        mixed[:, pl.ds(head * size, size)] = dot_nn(probs, values).astype(BF16)
    copies[-1].wait()
    for span in spans(width, TILE):
        added = dot_nn(mixed[...], w_out[:, span])
        h1_ref[:, span] = (rows_ref[:, span].astype(F32) + added).astype(BF16)
    for out in outs:
        out.wait()


def temporal_backward(
    gain_ref, grad_ref, rows_hbm, qkv_hbm, probs_hbm, w_qkv_hbm, w_out_hbm, out_ref,
    rows_ref, qkv_ref, probs_ref, w_qkv, w_out, grad_mixed, grad_qkv, grad_normed, sems,
):
    length, width = rows_ref.shape
    size = width // HEADS
    scale = 1.0 / math.sqrt(size)
    tiles = width // TILE

    def rows_of(step):
        return pl.ds(pl.multiple_of(step * TILE, TILE), TILE)

    def w_out_copy(step):
        return pltpu.make_async_copy(
            w_out_hbm.at[rows_of(step), :], w_out.at[rows_of(step), :], sems.at[step]
        )

    def w_qkv_copy(step):
        return pltpu.make_async_copy(
            w_qkv_hbm.at[rows_of(step), :], w_qkv.at[rows_of(step), :], sems.at[tiles + step]
        )

    qkv_copy = pltpu.make_async_copy(qkv_hbm, qkv_ref, sems.at[2 * tiles])
    probs_copy = pltpu.make_async_copy(probs_hbm, probs_ref, sems.at[2 * tiles + 1])
    rows_copy = pltpu.make_async_copy(rows_hbm, rows_ref, sems.at[2 * tiles + 2])
    for step in range(tiles):
        w_out_copy(step).start()
    qkv_copy.start()
    probs_copy.start()

    @pl.loop(0, tiles)
    def _(step):
        w_out_copy(step).wait()
        grad_mixed[:, rows_of(step)] = dot_nt(grad_ref[...], w_out[rows_of(step), :]).astype(BF16)

    for step in range(tiles):
        w_qkv_copy(step).start()
    rows_copy.start()
    qkv_copy.wait()
    probs_copy.wait()

    for head in range(HEADS):
        query_span = pl.ds(head * size, size)
        key_span = pl.ds(width + head * size, size)
        value_span = pl.ds(2 * width + head * size, size)
        probs = probs_ref[head]
        head_grad = grad_mixed[:, query_span]
        grad_qkv[:, value_span] = dot_tn(probs, head_grad).astype(BF16)
        grad_probs = dot_nt(head_grad, qkv_ref[:, value_span])
        wide = probs.astype(F32)
        inner = jnp.sum(wide * grad_probs, axis=-1, keepdims=True)
        grad_scores = (wide * (grad_probs - inner) * scale).astype(BF16)
        grad_qkv[:, query_span] = dot_nn(grad_scores, qkv_ref[:, key_span]).astype(BF16)
        grad_qkv[:, key_span] = dot_tn(grad_scores, qkv_ref[:, query_span]).astype(BF16)

    @pl.loop(0, tiles)
    def _(step):
        w_qkv_copy(step).wait()
        grad_normed[:, rows_of(step)] = dot_nt(grad_qkv[...], w_qkv[rows_of(step), :])

    rows_copy.wait()
    rows = rows_ref[...].astype(F32)
    pulled = norm_pull(rows, gain_ref[...], grad_normed[...])
    out_ref[...] = (grad_ref[...].astype(F32) + pulled).astype(BF16)


def agent_kernel(
    blocks, group_steps, env_ref, tm_ref, rows_ref, alive_ref, target_ref, gain_ref, value_ref,
    shard_ref, own_ref, *rest,
):
    moved = rest[: 2 * blocks]
    grad_ref, pack_ref, keep_ref, extra_ref, u_ref, predicted_ref = rest[2 * blocks : 2 * blocks + 6]
    w_all, qk, grad_qk, probs_all, slopes, column, grad_normed, sems = rest[2 * blocks + 6 :]
    total_rows, width = rows_ref.shape
    size = width // HEADS
    scale = 1.0 / math.sqrt(size)
    normed_ref = pack_ref.at[pl.ds(0, total_rows), :]
    groups, group_rows = alive_ref.shape[0], alive_ref.shape[2]
    agents = group_rows // group_steps
    local_steps = total_rows // agents
    depth, block_width = own_ref.shape
    middle = width // 2
    w_q, w_k = w_all.at[:, pl.ds(0, width)], w_all.at[:, pl.ds(block_width, width)]
    w_v = [
        w_all.at[:, pl.ds(width, middle)],
        w_all.at[:, pl.ds(block_width + width, middle)],
    ]
    core = core_of(env_ref)
    other = 1 - core
    near = blocks // 2
    far = blocks - near
    own_hops = [-hop for hop in range(1, far + 1)] + list(range(1, near + 1))
    hops = own_hops + [-hop for hop in own_hops]

    def row_span(hop):
        place = place_of(env_ref, tm_ref, blocks + 1, hop)
        return pl.ds(pl.multiple_of(place * depth, depth), depth)

    def column_span(start, length):
        return pl.ds(pl.multiple_of(start, 128), length)

    own_rows = row_span(0)
    other_at = other * block_width
    moves = [
        (own_ref, w_all.at[own_rows, column_span(core * block_width, block_width)]),
        (
            own_ref.at[:, pl.ds(block_width - 128, 128)],
            w_all.at[own_rows, column_span(other_at + block_width - 128, 128)],
        ),
        (
            shard_ref.at[:, column_span(other * width, width)],
            w_all.at[own_rows, column_span(other_at, width)],
        ),
        (
            shard_ref.at[:, column_span(2 * width + other * middle, middle)],
            w_all.at[own_rows, column_span(other_at + width, middle)],
        ),
    ]
    for at in range(2 * blocks):
        half = core if at < blocks else other
        moves.append(
            (moved[at], w_all.at[row_span(hops[at]), column_span(half * block_width, block_width)])
        )
    copies = started(moves, sems)

    def row_spans(group):
        if groups == 1:
            return [(pl.ds(0, total_rows), pl.ds(0, total_rows))]
        return [
            (
                pl.ds(agent * local_steps + group * group_steps, group_steps),
                pl.ds(group * group_rows + agent * group_steps, group_steps),
            )
            for agent in range(agents)
        ]

    def to_column(row):
        return jnp.transpose(jnp.broadcast_to(row, (128, row.shape[1])))[:, :1]

    for group in range(groups):
        for source, target in row_spans(group):
            rows = rows_ref[source, :].astype(F32)
            normed_ref[target, :] = (rows * inv_rms(rows) * gain_ref[...]).astype(BF16)
            column[target, :] = jnp.broadcast_to(
                jnp.sum(rows * value_ref[...], axis=-1, keepdims=True), (rows.shape[0], 128)
            )
    for copy in copies:
        copy.wait()

    u_parts = jnp.transpose(w_all[:, pl.ds(block_width - 128, 128)].astype(F32))
    u_high, u_low = u_parts[0:1], u_parts[1:2]
    u_ref[...] = u_high + u_low
    part_at = lax.broadcasted_iota(jnp.int32, (2 * HEADS, width), 0)
    head_at = lax.broadcasted_iota(jnp.int32, (2 * HEADS, width), 1) // size
    by_head = jnp.where(
        head_at == part_at % HEADS, jnp.where(part_at < HEADS, u_high, u_low), 0.0
    ).astype(BF16)
    both = dot_nt(by_head[:, :middle], w_v[0][...]) + dot_nt(by_head[:, middle:], w_v[1][...])
    folded = both[:HEADS] + both[HEADS:]
    folded_high = folded.astype(BF16)
    folded_parts = jnp.concatenate(
        [folded_high.astype(F32), folded - folded_high.astype(F32)], axis=0
    ).astype(BF16)
    both = dot_nt(folded_parts, normed_ref[...])
    folded_rows = both[:HEADS] + both[HEADS:]
    for at in range(0, width, TILE):
        qk[:, pl.ds(at, TILE)] = dot_nn(normed_ref[...], w_q[:, pl.ds(at, TILE)]).astype(BF16)
    for at in range(0, width, TILE):
        qk[:, pl.ds(width + at, TILE)] = dot_nn(
            normed_ref[...], w_k[:, pl.ds(at, TILE)]
        ).astype(BF16)

    row_at = lax.broadcasted_iota(jnp.int32, (group_rows, group_rows), 0)
    col_at = lax.broadcasted_iota(jnp.int32, (group_rows, group_rows), 1)
    same_step = row_at % group_steps == col_at % group_steps
    pulls = []
    for group in range(groups):
        group_span = pl.ds(group * group_rows, group_rows)
        alive = alive_ref[group]
        allowed = same_step & ((alive > 0.5) | (row_at == col_at))
        bias = jnp.where(allowed, 0.0, -1e30)
        predicted = column[group_span, :1]
        for head in range(HEADS):
            queries = qk[group_span, pl.ds(head * size, size)]
            keys = qk[group_span, pl.ds(width + head * size, size)]
            scores = dot_nt(queries, keys) * scale + bias
            weights = jnp.exp(scores - jnp.max(scores, axis=-1, keepdims=True))
            probs = weights * (1.0 / jnp.sum(weights, axis=-1, keepdims=True))
            weighted = probs * folded_rows[
                head : head + 1, group * group_rows : (group + 1) * group_rows
            ]
            pooled = jnp.sum(weighted, axis=-1, keepdims=True)
            predicted = predicted + pooled
            probs_all[group * HEADS + head] = probs
            slopes[group * HEADS + head] = (weighted - probs * pooled) * scale
        error = 32.0 * to_column(alive) * (predicted - to_column(target_ref[group]))
        predicted_ref[group] = jnp.transpose(jnp.broadcast_to(predicted, (group_rows, 128)))[:8]
        column[group_span, :] = jnp.broadcast_to(error, (group_rows, 128))
        pull_rows = []
        for head in range(HEADS):
            query_span = pl.ds(head * size, size)
            key_span = pl.ds(width + head * size, size)
            grad_scores = (slopes[group * HEADS + head] * error).astype(BF16)
            grad_qk[group_span, query_span] = dot_nn(
                grad_scores, qk[group_span, key_span]
            ).astype(BF16)
            grad_qk[group_span, key_span] = dot_tn(
                grad_scores, qk[group_span, query_span]
            ).astype(BF16)
            pull_rows.append(
                jnp.sum(probs_all[group * HEADS + head] * error, axis=0, keepdims=True)
            )
        pulls.append(jnp.concatenate(pull_rows, axis=0))
    pull = jnp.concatenate(pulls, axis=1) if groups > 1 else pulls[0]
    pull = pull.astype(BF16)
    twice = jnp.concatenate([pull, pull], axis=0)
    for at in range(0, width, TILE):
        span = pl.ds(at, TILE)
        grad_normed[:, span] = (
            dot_nt(grad_qk[:, pl.ds(0, width)], w_q[span, :])
            + dot_nt(grad_qk[:, pl.ds(width, width)], w_k[span, :])
            + dot_tn(twice, folded_parts[:, at : at + TILE])
        )
    for group in range(groups):
        for source, target in row_spans(group):
            rows = rows_ref[source, :].astype(F32)
            pulled = norm_pull(rows, gain_ref[...], grad_normed[target, :])
            top = column[target, :1] * value_ref[...]
            grad_ref[source, :] = (top + pulled).astype(BF16)
    keep_ref[...] = grad_qk[:, column_span(core * width, width)]
    pack_ref[pl.ds(total_rows, total_rows), :] = grad_qk[:, column_span(other * width, width)]

    folded_grad = dot_nn(pull, normed_ref[...])
    folded_grad_low = folded_grad.astype(BF16)
    pooled = jnp.concatenate(
        [dot_nn(folded_grad_low, w_v[0][...]), dot_nn(folded_grad_low, w_v[1][...])], axis=1
    )
    pooled = jnp.sum(
        jnp.where(head_at[:HEADS] == part_at[:HEADS], pooled, 0.0), axis=0, keepdims=True
    )
    extra = jnp.concatenate(
        [folded_grad, pooled, jnp.zeros((127 - HEADS, width), F32)], axis=0
    )
    extra_ref[...] = jnp.transpose(extra).astype(BF16)


def weight_grad_kernel(hops, env_ref, tm_ref, pack_ref, keep_ref, moved_ref, extra_ref, *rest):
    outs, (total, sems) = rest[:-2], rest[-2:]
    half, width = keep_ref.shape
    depth = width // len(outs)
    own, other = pl.ds(0, half), pl.ds(half, half)
    total[:, pl.ds(width, 128)] = extra_ref[...]
    for rows in spans(width, TILE):
        for columns in spans(width, TILE):
            total[rows, columns] = (
                dot_tn(pack_ref[own, rows], keep_ref[:, columns])
                + dot_tn(moved_ref[own, rows], moved_ref[other, columns])
            ).astype(BF16)
    copies = [
        pltpu.make_async_copy(
            total.at[
                pl.ds(
                    pl.multiple_of(place_of(env_ref, tm_ref, len(outs), hop) * depth, depth), depth
                ),
                :,
            ],
            out,
            sems.at[at],
        )
        for at, (hop, out) in enumerate(zip(hops, outs))
    ]
    for copy in copies:
        copy.start()
    for copy in copies:
        copy.wait()


def pack_block_kernel(env_ref, qk_ref, v_ref, w_out_ref, value_ref, out_ref):
    width, middle = qk_ref.shape[1], v_ref.shape[1]
    out_ref[:, pl.ds(0, width)] = qk_ref[...]
    out_ref[:, pl.ds(width, middle)] = v_ref[...]
    u = jnp.sum(w_out_ref[...].astype(F32) * value_ref[...], axis=-1, keepdims=True)
    high = u.astype(BF16).astype(F32)
    lane = lax.broadcasted_iota(jnp.int32, (qk_ref.shape[0], 128), 1)
    parts = jnp.where(lane == 0, high, jnp.where(lane == 1, u - high, 0.0))
    out_ref[:, pl.ds(width + middle, 128)] = parts.astype(BF16)


def finish_kernel(env_ref, own_ref, other_ref, u_ref, value_ref, qkv_ref, out_ref):
    width = u_ref.shape[1]
    size = width // HEADS
    own, other = own_ref[:, pl.ds(0, width)], other_ref[:, pl.ds(0, width)]
    core = core_of(env_ref)
    qkv_ref[:, pl.ds(pl.multiple_of(core * width, width), width)] = own.astype(F32)
    qkv_ref[:, pl.ds(pl.multiple_of((1 - core) * width, width), width)] = other.astype(F32)
    extra = own_ref[:, pl.ds(width, 128)].astype(F32) + other_ref[:, pl.ds(width, 128)].astype(F32)
    for head in range(HEADS):
        qkv_ref[:, pl.ds(2 * width + head * size, size)] = (
            extra[:, head : head + 1] * u_ref[:, pl.ds(head * size, size)]
        )
    out_ref[...] = extra[:, HEADS : HEADS + 1] * value_ref[...]


def any_spec():
    return pl.BlockSpec(memory_space=pl.ANY)


def hbm_spec():
    return pl.BlockSpec(memory_space=pltpu.HBM)


def vmem_spec():
    return pl.BlockSpec(memory_space=pltpu.VMEM)


def smem_spec():
    return pl.BlockSpec(memory_space=pltpu.SMEM)


def params():
    return pltpu.CompilerParams(vmem_limit_bytes=VMEM_BYTES)


def cost(flops, moved):
    return pl.CostEstimate(flops=flops, bytes_accessed=moved, transcendentals=0)


def ring_order(count):
    return list(range(0, count, 2)) + list(range(count - 1, 0, -2))


def per_device(
    env_count, tm_count,
    hidden, done_step, alive, targets, gain_t, w_qkv_t, w_out_t, gain_a, w_qkv_a, w_out_a, w_value,
):
    length, width = hidden.shape[2:]
    agents, local_steps = alive.shape[1:]
    depth = w_qkv_a.shape[0]
    env_index = lax.axis_index("env").astype(jnp.int32)[None]
    tm_index = lax.axis_index("tm").astype(jnp.int32)[None]
    order = ring_order(tm_count)
    spot = [order.index(at) for at in range(tm_count)]

    ways = [1 if at in (0, 3) else -1 for at in range(env_count)]

    def ring(block):
        pairs = [
            (env * tm_count + at, env * tm_count + order[(spot[at] + ways[env]) % tm_count])
            for env in range(env_count)
            for at in range(tm_count)
        ]
        return lax.ppermute(block, ("env", "tm"), pairs)

    def swap_core(block):
        return lax.ppermute(block, "env", [(at, at ^ 1) for at in range(env_count)])

    def swap_chip(block):
        return lax.ppermute(block, "env", [(at, at ^ 2) for at in range(env_count)])

    far = tm_count // 2
    near = tm_count - 1 - far

    block_width = width + width // 2 + 128
    own_block = pl.pallas_call(
        pack_block_kernel,
        name="pack_block",
        out_shape=jax.ShapeDtypeStruct((depth, block_width), BF16),
        grid_spec=pltpu.PrefetchScalarGridSpec(
            num_scalar_prefetch=1,
            grid=(1,),
            in_specs=[
                pl.BlockSpec((depth, width), lambda at, env: (0, core_of(env))),
                pl.BlockSpec((depth, width // 2), lambda at, env: (0, 4 + core_of(env))),
                pl.BlockSpec((depth, width), lambda at, env: (0, 0)),
                pl.BlockSpec((1, width), lambda at, env: (0, 0)),
            ],
            out_specs=pl.BlockSpec((depth, block_width), lambda at, env: (0, 0)),
        ),
        compiler_params=params(),
        cost_estimate=cost(2 * depth * width, 8 * depth * width),
    )(env_index, w_qkv_a, w_qkv_a, w_out_a, w_value[None])
    first_block = ring(own_block)

    rows = hidden[0, 0]
    h1, qkv, probs = pl.pallas_call(
        temporal_forward,
        name="temporal_forward",
        out_shape=(
            jax.ShapeDtypeStruct((length, width), BF16),
            jax.ShapeDtypeStruct((length, 3 * width), BF16),
            jax.ShapeDtypeStruct((HEADS, length, length), BF16),
        ),
        in_specs=[smem_spec()] + [vmem_spec()] * 2 + [hbm_spec()] * 2,
        out_specs=[vmem_spec()] + [hbm_spec()] * 2,
        scratch_shapes=[
            pltpu.VMEM((width, 3 * width), BF16),
            pltpu.VMEM((width, width), BF16),
            pltpu.VMEM((length, 3 * width), BF16),
            pltpu.VMEM((HEADS, length, length), BF16),
            pltpu.VMEM((length, width), BF16),
            pltpu.SemaphoreType.DMA((7,)),
            pltpu.SemaphoreType.DMA((HEADS + 1,)),
        ],
        compiler_params=params(),
        cost_estimate=cost(8 * length * width * width, 8 * width * width),
    )(done_step[0], rows, gain_t[None], w_qkv_t, w_out_t)
    h1, first_block = lax.optimization_barrier((h1, first_block))
    lifted = lax.all_to_all(h1, "tm", split_axis=0, concat_axis=0, tiled=True)

    ringed, crossed = [first_block], []
    for hop in range(1, far):
        if len(crossed) > 0:
            ringed[-1], crossed[-1] = lax.optimization_barrier((ringed[-1], crossed[-1]))
        if hop <= near:
            crossed.append(swap_chip(ringed[-1]))
        ringed.append(ring(ringed[-1]))
    crossed += [swap_chip(block) for block in ringed[len(crossed) : near]]
    own_blocks = ringed + crossed
    gated = far + near // 2
    lifted, own_blocks[gated] = lax.optimization_barrier((lifted, own_blocks[gated]))
    other_blocks = [swap_core(block) for block in own_blocks]

    group_steps = 16 if local_steps % 16 == 0 else local_steps
    groups = local_steps // group_steps
    group_rows = agents * group_steps

    def grouped(block):
        block = block.reshape(agents, groups, group_steps)
        return jnp.swapaxes(block, 0, 1).reshape(groups, 1, group_rows)

    total_rows = agents * local_steps
    grad_lifted, pack, keep, extra, u, predicted = pl.pallas_call(
        functools.partial(agent_kernel, tm_count - 1, group_steps),
        name="agent_block",
        out_shape=(
            jax.ShapeDtypeStruct((total_rows, width), BF16),
            jax.ShapeDtypeStruct((2 * total_rows, width), BF16),
            jax.ShapeDtypeStruct((total_rows, width), BF16),
            jax.ShapeDtypeStruct((width, 128), BF16),
            jax.ShapeDtypeStruct((1, width), F32),
            jax.ShapeDtypeStruct((groups, 8, group_rows), F32),
        ),
        in_specs=[smem_spec()] * 2 + [vmem_spec()] * 5 + [hbm_spec()] * (2 * tm_count),
        out_specs=[vmem_spec()] * 6,
        scratch_shapes=[
            pltpu.VMEM((width, 2 * block_width), BF16),
            pltpu.VMEM((total_rows, 2 * width), BF16),
            pltpu.VMEM((total_rows, 2 * width), BF16),
            pltpu.VMEM((groups * HEADS, group_rows, group_rows), F32),
            pltpu.VMEM((groups * HEADS, group_rows, group_rows), F32),
            pltpu.VMEM((total_rows, 128), F32),
            pltpu.VMEM((total_rows, width), F32),
            pltpu.SemaphoreType.DMA((2 * tm_count + 2,)),
        ],
        compiler_params=params(),
        cost_estimate=cost(8 * total_rows * width * width, 4 * width * width),
    )(
        env_index, tm_index, lifted, grouped(alive[0].astype(F32)), grouped(targets[0]), gain_a[None],
        w_value[None], w_qkv_a, own_block, *own_blocks, *other_blocks,
    )
    values = predicted[:, 0].reshape(groups, agents, group_steps)
    values = jnp.swapaxes(values, 0, 1).reshape(1, agents, local_steps)

    returned = lax.all_to_all(grad_lifted, "tm", split_axis=0, concat_axis=0, tiled=True)

    moved = swap_core(pack)
    hops = list(range(far + 1)) + [-hop for hop in range(1, near + 1)]
    terms = pl.pallas_call(
        functools.partial(weight_grad_kernel, hops),
        name="weight_grad",
        out_shape=[jax.ShapeDtypeStruct((depth, width + 128), BF16)] * tm_count,
        in_specs=[smem_spec()] * 2 + [vmem_spec()] * 4,
        out_specs=[hbm_spec()] * tm_count,
        scratch_shapes=[
            pltpu.VMEM((width, width + 128), BF16),
            pltpu.SemaphoreType.DMA((tm_count,)),
        ],
        compiler_params=params(),
        cost_estimate=cost(4 * total_rows * width * width, 4 * width * width),
    )(env_index, tm_index, pack, keep, moved, extra)
    def temporal_gradient(returned):
        return pl.pallas_call(
            temporal_backward,
            name="temporal_backward",
            out_shape=jax.ShapeDtypeStruct((length, width), BF16),
            in_specs=[vmem_spec()] * 2 + [hbm_spec()] * 5,
            out_specs=vmem_spec(),
            scratch_shapes=[
                pltpu.VMEM((length, width), BF16),
                pltpu.VMEM((length, 3 * width), BF16),
                pltpu.VMEM((HEADS, length, length), BF16),
                pltpu.VMEM((width, 3 * width), BF16),
                pltpu.VMEM((width, width), BF16),
                pltpu.VMEM((length, width), BF16),
                pltpu.VMEM((length, 3 * width), BF16),
                pltpu.VMEM((length, width), F32),
                pltpu.SemaphoreType.DMA((3 + 2 * (width // TILE),)),
            ],
            compiler_params=params(),
            cost_estimate=cost(8 * length * width * width, 8 * width * width),
        )(gain_t[None], returned, rows, qkv, probs, w_qkv_t, w_out_t)

    term = dict(zip(hops, terms))
    travelling = ring(term[far])
    chip_term = swap_chip(term[-near])
    for hop in range(far - 1, 0, -1):
        if hop > 1:
            following, chip_term = lax.optimization_barrier((term[1 - hop], chip_term))
            next_chip_term = swap_chip(following)
        if hop == 2:
            travelling, returned = lax.optimization_barrier((travelling, returned))
        if hop == 1:
            input_grad = temporal_gradient(returned)
            travelling, input_grad = lax.optimization_barrier((travelling, input_grad))
        total = travelling.astype(F32) + term[hop].astype(F32) + chip_term.astype(F32)
        travelling = ring(total.astype(BF16))
        chip_term = next_chip_term
    reduced = (travelling.astype(F32) + term[0].astype(F32)).astype(BF16)
    reduced = (reduced.astype(F32) + swap_chip(reduced).astype(F32)).astype(BF16)
    reduced, values = lax.optimization_barrier((reduced, values))
    other = swap_core(reduced)
    qkv_grad, out_grad = pl.pallas_call(
        finish_kernel,
        name="finish",
        out_shape=(
            jax.ShapeDtypeStruct((depth, 3 * width), F32),
            jax.ShapeDtypeStruct((depth, width), F32),
        ),
        in_specs=[smem_spec()] + [vmem_spec()] * 4,
        out_specs=[vmem_spec()] * 2,
        compiler_params=params(),
        cost_estimate=cost(8 * depth * width, 20 * depth * width),
    )(env_index, reduced, other, u, w_value[None])
    return values, input_grad[None, None], qkv_grad, out_grad


def solution(mesh):
    in_specs = (
        P("env", "tm", None, None),
        P("env", "tm"),
        P("env", None, "tm"),
        P("env", None, "tm"),
        P(),
        P(),
        P(),
        P(),
        P("tm", None),
        P("tm", None),
        P(),
    )
    out_specs = (P("env", None, "tm"), P("env", "tm", None, None), P("tm", None), P("tm", None))
    body = functools.partial(per_device, mesh.shape["env"], mesh.shape["tm"])
    return jax.shard_map(
        body, mesh=mesh, in_specs=in_specs, out_specs=out_specs, check_vma=False
    )
```

```python
import functools
import math

import jax
import jax.numpy as jnp
from jax import lax
from jax.experimental import pallas as pl
from jax.experimental.pallas import tpu as pltpu
from jax.sharding import PartitionSpec as P

HEADS = 8
EPS = 1e-06
F32 = jnp.float32
BF16 = jnp.bfloat16
TILE = 256


def dot_nn(a, b):
    return lax.dot_general(a, b, (((1,), (0,)), ((), ())), preferred_element_type=F32)


def dot_nt(a, b):
    return lax.dot_general(a, b, (((1,), (1,)), ((), ())), preferred_element_type=F32)


def dot_tn(a, b):
    return lax.dot_general(a, b, (((0,), (0,)), ((), ())), preferred_element_type=F32)


def inv_rms(rows):
    return lax.rsqrt(jnp.mean(rows * rows, axis=-1, keepdims=True) + EPS)


def norm_pull(rows, gain, grad):
    scale = inv_rms(rows)
    scaled = grad * gain
    inner = jnp.mean(scaled * rows, axis=-1, keepdims=True)
    return scale * scaled - rows * (scale * scale * scale * inner)


def spans(total, size):
    size = min(size, total)
    return [pl.ds(at, size) for at in range(0, total, size)]


def core_of(env_ref):
    return env_ref[0] % 2


def place_of(env_ref, tm_ref, count, hop):
    at = tm_ref[0]
    way = 1 - 2 * ((env_ref[0] + env_ref[0] // 2) % 2)
    spot = jnp.where(at % 2 == 0, at // 2, count - 1 - at // 2)
    spot = (spot + way * hop + count) % count
    return jnp.where(spot < count // 2, 2 * spot, 2 * (count - 1 - spot) + 1)


def copies_of(moves, sems):
    return [
        pltpu.make_async_copy(source, target, sems.at[at])
        for at, (source, target) in enumerate(moves)
    ]


def started(moves, sems):
    copies = copies_of(moves, sems)
    for copy in copies:
        copy.start()
    return copies


def temporal_forward(
    done_ref, rows_ref, gain_ref, w_qkv_hbm, w_out_hbm, h1_ref, qkv_hbm, probs_hbm,
    w_qkv, w_out, qkv_ref, probs_ref, mixed, sems, out_sems,
):
    length, width = rows_ref.shape
    size = width // HEADS
    chunks = spans(3 * width, width // 2)
    moves = [(w_qkv_hbm.at[:, span], w_qkv.at[:, span]) for span in chunks]
    copies = started(moves + [(w_out_hbm, w_out)], sems)
    rows = rows_ref[...].astype(F32)
    normed = (rows * inv_rms(rows) * gain_ref[...]).astype(BF16)
    outs = copies_of(
        [(qkv_ref, qkv_hbm)] + [(probs_ref.at[head], probs_hbm.at[head]) for head in range(HEADS)],
        out_sems,
    )
    for part, chunk in enumerate(chunks):
        copies[part].wait()
        for at in range(chunk.start, chunk.start + chunk.size, TILE):
            span = pl.ds(at, TILE)
            qkv_ref[:, span] = dot_nn(normed, w_qkv[:, span]).astype(BF16)
    outs[0].start()
    done = done_ref[0]
    query_at = lax.broadcasted_iota(jnp.int32, (length, length), 0)
    key_at = lax.broadcasted_iota(jnp.int32, (length, length), 1)
    allowed = (key_at <= query_at) & ((key_at > done) == (query_at > done))
    bias = jnp.where(allowed, 0.0, -1e30)
    for head in range(HEADS):
        queries = qkv_ref[:, pl.ds(head * size, size)]
        keys = qkv_ref[:, pl.ds(width + head * size, size)]
        values = qkv_ref[:, pl.ds(2 * width + head * size, size)]
        scores = dot_nt(queries, keys) * (1.0 / math.sqrt(size)) + bias
        weights = jnp.exp(scores - jnp.max(scores, axis=-1, keepdims=True))
        probs = weights * (1.0 / jnp.sum(weights, axis=-1, keepdims=True))
        probs = probs.astype(BF16)
        probs_ref[head] = probs
        outs[1 + head].start()
        mixed[:, pl.ds(head * size, size)] = dot_nn(probs, values).astype(BF16)
    copies[-1].wait()
    for span in spans(width, TILE):
        added = dot_nn(mixed[...], w_out[:, span])
        h1_ref[:, span] = (rows_ref[:, span].astype(F32) + added).astype(BF16)
    for out in outs:
        out.wait()


def mix_grad_kernel(
    first_head, grad_ref, w_hbm, qkv_hbm, probs_hbm, out_ref, w_ref, qkv_ref, probs_ref,
    grad_mixed, sems,
):
    length, width = grad_ref.shape
    size = width // HEADS
    heads, part = probs_ref.shape[0], out_ref.shape[1] // 3
    scale = 1.0 / math.sqrt(size)
    tiles, start = part // TILE, first_head * size

    def w_copy(step):
        source = pl.ds(pl.multiple_of(start + step * TILE, TILE), TILE)
        target = pl.ds(pl.multiple_of(step * TILE, TILE), TILE)
        return pltpu.make_async_copy(w_hbm.at[source, :], w_ref.at[target, :], sems.at[step])

    for step in range(tiles):
        w_copy(step).start()
    moves = [
        (qkv_hbm.at[:, pl.ds(at * width + start, part)], qkv_ref.at[:, pl.ds(at * part, part)])
        for at in range(3)
    ]
    moves.append((probs_hbm.at[pl.ds(first_head, heads)], probs_ref))
    copies = [
        pltpu.make_async_copy(source, target, sems.at[tiles + at])
        for at, (source, target) in enumerate(moves)
    ]
    for copy in copies:
        copy.start()

    @pl.loop(0, tiles)
    def _(step):
        w_copy(step).wait()
        span = pl.ds(pl.multiple_of(step * TILE, TILE), TILE)
        grad_mixed[:, span] = dot_nt(grad_ref[...], w_ref[span, :]).astype(BF16)

    for copy in copies:
        copy.wait()
    for head in range(heads):
        query_span = pl.ds(head * size, size)
        key_span = pl.ds(part + head * size, size)
        value_span = pl.ds(2 * part + head * size, size)
        probs = probs_ref[head]
        head_grad = grad_mixed[:, query_span]
        out_ref[:, value_span] = dot_tn(probs, head_grad).astype(BF16)
        grad_probs = dot_nt(head_grad, qkv_ref[:, value_span])
        wide = probs.astype(F32)
        inner = jnp.sum(wide * grad_probs, axis=-1, keepdims=True)
        grad_scores = (wide * (grad_probs - inner) * scale).astype(BF16)
        out_ref[:, query_span] = dot_nn(grad_scores, qkv_ref[:, key_span]).astype(BF16)
        out_ref[:, key_span] = dot_tn(grad_scores, qkv_ref[:, query_span]).astype(BF16)


def norm_grad_kernel(
    gain_ref, grad_ref, rows_ref, low_ref, high_ref, w_hbm, out_ref, w_ref, grad_normed, sems
):
    width = rows_ref.shape[1]
    tiles, part = width // TILE, low_ref.shape[1] // 3

    def rows_of(step):
        return pl.ds(pl.multiple_of(step * TILE, TILE), TILE)

    def w_copy(step):
        return pltpu.make_async_copy(
            w_hbm.at[rows_of(step), :], w_ref.at[rows_of(step), :], sems.at[step]
        )

    for step in range(tiles):
        w_copy(step).start()

    @pl.loop(0, tiles)
    def _(step):
        w_copy(step).wait()
        total = None
        for side, grads_ref in enumerate((low_ref, high_ref)):
            for at in range(3):
                columns = pl.ds(at * width + side * part, part)
                product = dot_nt(grads_ref[:, pl.ds(at * part, part)], w_ref[rows_of(step), columns])
                total = product if total is None else total + product
        grad_normed[:, rows_of(step)] = total

    rows = rows_ref[...].astype(F32)
    pulled = norm_pull(rows, gain_ref[...], grad_normed[...])
    out_ref[...] = (grad_ref[...].astype(F32) + pulled).astype(BF16)


def agent_kernel(
    blocks, group_steps, env_ref, tm_ref, rows_ref, alive_ref, target_ref, gain_ref, value_ref,
    shard_ref, own_ref, *rest,
):
    moved = rest[: 2 * blocks]
    grad_ref, pack_ref, keep_ref, extra_ref, u_ref, predicted_ref = rest[2 * blocks : 2 * blocks + 6]
    w_all, qk, grad_qk, probs_all, slopes, column, grad_normed, sems = rest[2 * blocks + 6 :]
    total_rows, width = rows_ref.shape
    size = width // HEADS
    scale = 1.0 / math.sqrt(size)
    normed_ref = pack_ref.at[pl.ds(0, total_rows), :]
    groups, group_rows = alive_ref.shape[0], alive_ref.shape[2]
    agents = group_rows // group_steps
    local_steps = total_rows // agents
    depth, block_width = own_ref.shape
    middle = width // 2
    w_q, w_k = w_all.at[:, pl.ds(0, width)], w_all.at[:, pl.ds(block_width, width)]
    w_v = [
        w_all.at[:, pl.ds(width, middle)],
        w_all.at[:, pl.ds(block_width + width, middle)],
    ]
    core = core_of(env_ref)
    other = 1 - core
    near = blocks // 2
    far = blocks - near
    own_hops = [-hop for hop in range(1, far + 1)] + list(range(1, near + 1))
    hops = own_hops + [-hop for hop in own_hops]

    def row_span(hop):
        place = place_of(env_ref, tm_ref, blocks + 1, hop)
        return pl.ds(pl.multiple_of(place * depth, depth), depth)

    def column_span(start, length):
        return pl.ds(pl.multiple_of(start, 128), length)

    own_rows = row_span(0)
    other_at = other * block_width
    moves = [
        (own_ref, w_all.at[own_rows, column_span(core * block_width, block_width)]),
        (
            own_ref.at[:, pl.ds(block_width - 128, 128)],
            w_all.at[own_rows, column_span(other_at + block_width - 128, 128)],
        ),
        (
            shard_ref.at[:, column_span(other * width, width)],
            w_all.at[own_rows, column_span(other_at, width)],
        ),
        (
            shard_ref.at[:, column_span(2 * width + other * middle, middle)],
            w_all.at[own_rows, column_span(other_at + width, middle)],
        ),
    ]
    for at in range(2 * blocks):
        half = core if at < blocks else other
        moves.append(
            (moved[at], w_all.at[row_span(hops[at]), column_span(half * block_width, block_width)])
        )
    copies = started(moves, sems)

    def row_spans(group):
        if groups == 1:
            return [(pl.ds(0, total_rows), pl.ds(0, total_rows))]
        return [
            (
                pl.ds(agent * local_steps + group * group_steps, group_steps),
                pl.ds(group * group_rows + agent * group_steps, group_steps),
            )
            for agent in range(agents)
        ]

    def to_column(row):
        return jnp.transpose(jnp.broadcast_to(row, (128, row.shape[1])))[:, :1]

    for group in range(groups):
        for source, target in row_spans(group):
            rows = rows_ref[source, :].astype(F32)
            normed_ref[target, :] = (rows * inv_rms(rows) * gain_ref[...]).astype(BF16)
            column[target, :] = jnp.broadcast_to(
                jnp.sum(rows * value_ref[...], axis=-1, keepdims=True), (rows.shape[0], 128)
            )
    for copy in copies:
        copy.wait()

    u_parts = jnp.transpose(w_all[:, pl.ds(block_width - 128, 128)].astype(F32))
    u_high, u_low = u_parts[0:1], u_parts[1:2]
    u_ref[...] = u_high + u_low
    part_at = lax.broadcasted_iota(jnp.int32, (2 * HEADS, width), 0)
    head_at = lax.broadcasted_iota(jnp.int32, (2 * HEADS, width), 1) // size
    by_head = jnp.where(
        head_at == part_at % HEADS, jnp.where(part_at < HEADS, u_high, u_low), 0.0
    ).astype(BF16)
    both = dot_nt(by_head[:, :middle], w_v[0][...]) + dot_nt(by_head[:, middle:], w_v[1][...])
    folded = both[:HEADS] + both[HEADS:]
    folded_high = folded.astype(BF16)
    folded_parts = jnp.concatenate(
        [folded_high.astype(F32), folded - folded_high.astype(F32)], axis=0
    ).astype(BF16)
    both = dot_nt(folded_parts, normed_ref[...])
    folded_rows = both[:HEADS] + both[HEADS:]
    for at in range(0, width, TILE):
        qk[:, pl.ds(at, TILE)] = dot_nn(normed_ref[...], w_q[:, pl.ds(at, TILE)]).astype(BF16)
    for at in range(0, width, TILE):
        qk[:, pl.ds(width + at, TILE)] = dot_nn(
            normed_ref[...], w_k[:, pl.ds(at, TILE)]
        ).astype(BF16)

    row_at = lax.broadcasted_iota(jnp.int32, (group_rows, group_rows), 0)
    col_at = lax.broadcasted_iota(jnp.int32, (group_rows, group_rows), 1)
    same_step = row_at % group_steps == col_at % group_steps
    pulls = []
    for group in range(groups):
        group_span = pl.ds(group * group_rows, group_rows)
        alive = alive_ref[group]
        allowed = same_step & ((alive > 0.5) | (row_at == col_at))
        bias = jnp.where(allowed, 0.0, -1e30)
        predicted = column[group_span, :1]
        for head in range(HEADS):
            queries = qk[group_span, pl.ds(head * size, size)]
            keys = qk[group_span, pl.ds(width + head * size, size)]
            scores = dot_nt(queries, keys) * scale + bias
            weights = jnp.exp(scores - jnp.max(scores, axis=-1, keepdims=True))
            probs = weights * (1.0 / jnp.sum(weights, axis=-1, keepdims=True))
            weighted = probs * folded_rows[
                head : head + 1, group * group_rows : (group + 1) * group_rows
            ]
            pooled = jnp.sum(weighted, axis=-1, keepdims=True)
            predicted = predicted + pooled
            probs_all[group * HEADS + head] = probs
            slopes[group * HEADS + head] = (weighted - probs * pooled) * scale
        error = 32.0 * to_column(alive) * (predicted - to_column(target_ref[group]))
        predicted_ref[group] = jnp.transpose(jnp.broadcast_to(predicted, (group_rows, 128)))[:8]
        column[group_span, :] = jnp.broadcast_to(error, (group_rows, 128))
        pull_rows = []
        for head in range(HEADS):
            query_span = pl.ds(head * size, size)
            key_span = pl.ds(width + head * size, size)
            grad_scores = (slopes[group * HEADS + head] * error).astype(BF16)
            grad_qk[group_span, query_span] = dot_nn(
                grad_scores, qk[group_span, key_span]
            ).astype(BF16)
            grad_qk[group_span, key_span] = dot_tn(
                grad_scores, qk[group_span, query_span]
            ).astype(BF16)
            pull_rows.append(
                jnp.sum(probs_all[group * HEADS + head] * error, axis=0, keepdims=True)
            )
        pulls.append(jnp.concatenate(pull_rows, axis=0))
    pull = jnp.concatenate(pulls, axis=1) if groups > 1 else pulls[0]
    pull = pull.astype(BF16)
    twice = jnp.concatenate([pull, pull], axis=0)
    for at in range(0, width, TILE):
        span = pl.ds(at, TILE)
        grad_normed[:, span] = (
            dot_nt(grad_qk[:, pl.ds(0, width)], w_q[span, :])
            + dot_nt(grad_qk[:, pl.ds(width, width)], w_k[span, :])
            + dot_tn(twice, folded_parts[:, at : at + TILE])
        )
    for group in range(groups):
        for source, target in row_spans(group):
            rows = rows_ref[source, :].astype(F32)
            pulled = norm_pull(rows, gain_ref[...], grad_normed[target, :])
            top = column[target, :1] * value_ref[...]
            grad_ref[source, :] = (top + pulled).astype(BF16)
    keep_ref[...] = grad_qk[:, column_span(core * width, width)]
    pack_ref[pl.ds(total_rows, total_rows), :] = grad_qk[:, column_span(other * width, width)]

    folded_grad = dot_nn(pull, normed_ref[...])
    folded_grad_low = folded_grad.astype(BF16)
    pooled = jnp.concatenate(
        [dot_nn(folded_grad_low, w_v[0][...]), dot_nn(folded_grad_low, w_v[1][...])], axis=1
    )
    pooled = jnp.sum(
        jnp.where(head_at[:HEADS] == part_at[:HEADS], pooled, 0.0), axis=0, keepdims=True
    )
    extra = jnp.concatenate(
        [folded_grad, pooled, jnp.zeros((127 - HEADS, width), F32)], axis=0
    )
    extra_ref[...] = jnp.transpose(extra).astype(BF16)


def weight_grad_kernel(hops, env_ref, tm_ref, pack_ref, keep_ref, moved_ref, extra_ref, *rest):
    outs, (total, sems) = rest[:-2], rest[-2:]
    half, width = keep_ref.shape
    depth = width // len(outs)
    own, other = pl.ds(0, half), pl.ds(half, half)
    total[:, pl.ds(width, 128)] = extra_ref[...]
    for rows in spans(width, TILE):
        for columns in spans(width, TILE):
            total[rows, columns] = (
                dot_tn(pack_ref[own, rows], keep_ref[:, columns])
                + dot_tn(moved_ref[own, rows], moved_ref[other, columns])
            ).astype(BF16)
    copies = [
        pltpu.make_async_copy(
            total.at[
                pl.ds(
                    pl.multiple_of(place_of(env_ref, tm_ref, len(outs), hop) * depth, depth), depth
                ),
                :,
            ],
            out,
            sems.at[at],
        )
        for at, (hop, out) in enumerate(zip(hops, outs))
    ]
    for copy in copies:
        copy.start()
    for copy in copies:
        copy.wait()


def pack_block_kernel(env_ref, qk_ref, v_ref, w_out_ref, value_ref, out_ref):
    width, middle = qk_ref.shape[1], v_ref.shape[1]
    out_ref[:, pl.ds(0, width)] = qk_ref[...]
    out_ref[:, pl.ds(width, middle)] = v_ref[...]
    u = jnp.sum(w_out_ref[...].astype(F32) * value_ref[...], axis=-1, keepdims=True)
    high = u.astype(BF16).astype(F32)
    lane = lax.broadcasted_iota(jnp.int32, (qk_ref.shape[0], 128), 1)
    parts = jnp.where(lane == 0, high, jnp.where(lane == 1, u - high, 0.0))
    out_ref[:, pl.ds(width + middle, 128)] = parts.astype(BF16)


def finish_kernel(env_ref, own_ref, other_ref, u_ref, value_ref, qkv_ref, out_ref):
    width = u_ref.shape[1]
    size = width // HEADS
    own, other = own_ref[:, pl.ds(0, width)], other_ref[:, pl.ds(0, width)]
    core = core_of(env_ref)
    qkv_ref[:, pl.ds(pl.multiple_of(core * width, width), width)] = own.astype(F32)
    qkv_ref[:, pl.ds(pl.multiple_of((1 - core) * width, width), width)] = other.astype(F32)
    extra = own_ref[:, pl.ds(width, 128)].astype(F32) + other_ref[:, pl.ds(width, 128)].astype(F32)
    for head in range(HEADS):
        qkv_ref[:, pl.ds(2 * width + head * size, size)] = (
            extra[:, head : head + 1] * u_ref[:, pl.ds(head * size, size)]
        )
    out_ref[...] = extra[:, HEADS : HEADS + 1] * value_ref[...]


def any_spec():
    return pl.BlockSpec(memory_space=pl.ANY)


def hbm_spec():
    return pl.BlockSpec(memory_space=pltpu.HBM)


def vmem_spec():
    return pl.BlockSpec(memory_space=pltpu.VMEM)


def smem_spec():
    return pl.BlockSpec(memory_space=pltpu.SMEM)


def params(mebibytes=60):
    return pltpu.CompilerParams(vmem_limit_bytes=mebibytes * 1024 * 1024)


def cost(microseconds):
    return pl.CostEstimate(
        flops=int(microseconds * 1e9), bytes_accessed=int(microseconds * 2e6), transcendentals=0
    )


def ring_order(count):
    return list(range(0, count, 2)) + list(range(count - 1, 0, -2))


def per_device(
    env_count, tm_count,
    hidden, done_step, alive, targets, gain_t, w_qkv_t, w_out_t, gain_a, w_qkv_a, w_out_a, w_value,
):
    length, width = hidden.shape[2:]
    agents, local_steps = alive.shape[1:]
    depth = w_qkv_a.shape[0]
    env_index = lax.axis_index("env").astype(jnp.int32)[None]
    tm_index = lax.axis_index("tm").astype(jnp.int32)[None]
    order = ring_order(tm_count)
    spot = [order.index(at) for at in range(tm_count)]

    ways = [1 if at in (0, 3) else -1 for at in range(env_count)]

    def ring(block, along=1):
        pairs = [
            (env * tm_count + at, env * tm_count + order[(spot[at] + along * ways[env]) % tm_count])
            for env in range(env_count)
            for at in range(tm_count)
        ]
        return lax.ppermute(block, ("env", "tm"), pairs)

    def swap_core(block):
        return lax.ppermute(block, "env", [(at, at ^ 1) for at in range(env_count)])

    def swap_chip(block):
        return lax.ppermute(block, "env", [(at, at ^ 2) for at in range(env_count)])

    far = tm_count // 2
    near = tm_count - 1 - far

    block_width = width + width // 2 + 128
    own_block = pl.pallas_call(
        pack_block_kernel,
        name="pack_block",
        out_shape=jax.ShapeDtypeStruct((depth, block_width), BF16),
        grid_spec=pltpu.PrefetchScalarGridSpec(
            num_scalar_prefetch=1,
            grid=(1,),
            in_specs=[
                pl.BlockSpec((depth, width), lambda at, env: (0, core_of(env))),
                pl.BlockSpec((depth, width // 2), lambda at, env: (0, 4 + core_of(env))),
                pl.BlockSpec((depth, width), lambda at, env: (0, 0)),
                pl.BlockSpec((1, width), lambda at, env: (0, 0)),
            ],
            out_specs=pl.BlockSpec((depth, block_width), lambda at, env: (0, 0)),
        ),
        compiler_params=params(),
        cost_estimate=cost(2),
    )(env_index, w_qkv_a, w_qkv_a, w_out_a, w_value[None])
    first_block = ring(own_block)

    rows = hidden[0, 0]
    h1, qkv, probs = pl.pallas_call(
        temporal_forward,
        name="temporal_forward",
        out_shape=(
            jax.ShapeDtypeStruct((length, width), BF16),
            jax.ShapeDtypeStruct((length, 3 * width), BF16),
            jax.ShapeDtypeStruct((HEADS, length, length), BF16),
        ),
        in_specs=[smem_spec()] + [vmem_spec()] * 2 + [hbm_spec()] * 2,
        out_specs=[vmem_spec()] + [hbm_spec()] * 2,
        scratch_shapes=[
            pltpu.VMEM((width, 3 * width), BF16),
            pltpu.VMEM((width, width), BF16),
            pltpu.VMEM((length, 3 * width), BF16),
            pltpu.VMEM((HEADS, length, length), BF16),
            pltpu.VMEM((length, width), BF16),
            pltpu.SemaphoreType.DMA((7,)),
            pltpu.SemaphoreType.DMA((HEADS + 1,)),
        ],
        compiler_params=params(),
        cost_estimate=cost(8),
    )(done_step[0], rows, gain_t[None], w_qkv_t, w_out_t)
    h1, first_block = lax.optimization_barrier((h1, first_block))
    lifted = lax.all_to_all(h1, "tm", split_axis=0, concat_axis=0, tiled=True)

    ringed, crossed = [first_block], []
    for hop in range(1, far):
        if len(crossed) > 0:
            ringed[-1], crossed[-1] = lax.optimization_barrier((ringed[-1], crossed[-1]))
        if hop <= near:
            crossed.append(swap_chip(ringed[-1]))
        ringed.append(ring(ringed[-1]))
    crossed += [swap_chip(block) for block in ringed[len(crossed) : near]]
    own_blocks = ringed + crossed
    gated = far + near // 2
    lifted, own_blocks[gated] = lax.optimization_barrier((lifted, own_blocks[gated]))
    other_blocks = [swap_core(block) for block in own_blocks]

    group_steps = 16 if local_steps % 16 == 0 else local_steps
    groups = local_steps // group_steps
    group_rows = agents * group_steps

    def grouped(block):
        block = block.reshape(agents, groups, group_steps)
        return jnp.swapaxes(block, 0, 1).reshape(groups, 1, group_rows)

    total_rows = agents * local_steps
    grad_lifted, pack, keep, extra, u, predicted = pl.pallas_call(
        functools.partial(agent_kernel, tm_count - 1, group_steps),
        name="agent_block",
        out_shape=(
            jax.ShapeDtypeStruct((total_rows, width), BF16),
            jax.ShapeDtypeStruct((2 * total_rows, width), BF16),
            jax.ShapeDtypeStruct((total_rows, width), BF16),
            jax.ShapeDtypeStruct((width, 128), BF16),
            jax.ShapeDtypeStruct((1, width), F32),
            jax.ShapeDtypeStruct((groups, 8, group_rows), F32),
        ),
        in_specs=[smem_spec()] * 2 + [vmem_spec()] * 5 + [hbm_spec()] * (2 * tm_count),
        out_specs=[vmem_spec()] * 6,
        scratch_shapes=[
            pltpu.VMEM((width, 2 * block_width), BF16),
            pltpu.VMEM((total_rows, 2 * width), BF16),
            pltpu.VMEM((total_rows, 2 * width), BF16),
            pltpu.VMEM((groups * HEADS, group_rows, group_rows), F32),
            pltpu.VMEM((groups * HEADS, group_rows, group_rows), F32),
            pltpu.VMEM((total_rows, 128), F32),
            pltpu.VMEM((total_rows, width), F32),
            pltpu.SemaphoreType.DMA((2 * tm_count + 2,)),
        ],
        compiler_params=params(),
        cost_estimate=cost(11),
    )(
        env_index, tm_index, lifted, grouped(alive[0].astype(F32)), grouped(targets[0]), gain_a[None],
        w_value[None], w_qkv_a, own_block, *own_blocks, *other_blocks,
    )
    values = predicted[:, 0].reshape(groups, agents, group_steps)
    values = jnp.swapaxes(values, 0, 1).reshape(1, agents, local_steps)

    returned = lax.all_to_all(grad_lifted, "tm", split_axis=0, concat_axis=0, tiled=True)

    moved = swap_core(pack)
    hops = list(range(far + 1)) + [-hop for hop in range(1, near + 1)]
    terms = pl.pallas_call(
        functools.partial(weight_grad_kernel, hops),
        name="weight_grad",
        out_shape=[jax.ShapeDtypeStruct((depth, width + 128), BF16)] * tm_count,
        in_specs=[smem_spec()] * 2 + [vmem_spec()] * 4,
        out_specs=[any_spec()] * tm_count,
        scratch_shapes=[
            pltpu.VMEM((width, width + 128), BF16),
            pltpu.SemaphoreType.DMA((tm_count,)),
        ],
        compiler_params=params(20),
        cost_estimate=cost(4),
    )(env_index, tm_index, pack, keep, moved, extra)
    def mix_grad(first_head):
        heads, part = HEADS // 2, width // 2
        return pl.pallas_call(
            functools.partial(mix_grad_kernel, first_head),
            name="temporal_mix_grad",
            out_shape=jax.ShapeDtypeStruct((length, 3 * part), BF16),
            in_specs=[vmem_spec()] + [hbm_spec()] * 3,
            out_specs=vmem_spec(),
            scratch_shapes=[
                pltpu.VMEM((part, width), BF16),
                pltpu.VMEM((length, 3 * part), BF16),
                pltpu.VMEM((heads, length, length), BF16),
                pltpu.VMEM((length, part), BF16),
                pltpu.SemaphoreType.DMA((part // TILE + 4,)),
            ],
            compiler_params=params(),
            cost_estimate=cost(4),
        )(returned, w_out_t, qkv, probs)

    term = dict(zip(hops, terms))
    travelling = ring(term[far])
    chip_terms = {hop: swap_chip(term[-hop]) for hop in range(near, 1, -1)}
    arriving = ring(term[-1], -1)
    for hop in range(far - 1, 0, -1):
        if hop == far - 1:
            travelling, returned = lax.optimization_barrier((travelling, returned))
        if hop == max(far - 2, 1):
            travelling, low_grads, arriving = lax.optimization_barrier(
                (travelling, mix_grad(0), arriving)
            )
        if hop == max(far - 3, 1):
            travelling, high_grads = lax.optimization_barrier((travelling, mix_grad(HEADS // 2)))
        total = travelling.astype(F32) + term[hop].astype(F32)
        if hop in chip_terms:
            total = total + chip_terms[hop].astype(F32)
        travelling = ring(total.astype(BF16))
    input_grad = pl.pallas_call(
        norm_grad_kernel,
        name="temporal_norm_grad",
        out_shape=jax.ShapeDtypeStruct((length, width), BF16),
        in_specs=[vmem_spec()] * 5 + [hbm_spec()],
        out_specs=vmem_spec(),
        scratch_shapes=[
            pltpu.VMEM((width, 3 * width), BF16),
            pltpu.VMEM((length, width), F32),
            pltpu.SemaphoreType.DMA((width // TILE,)),
        ],
        compiler_params=params(),
        cost_estimate=cost(6),
    )(gain_t[None], returned, rows, low_grads, high_grads, w_qkv_t)
    reduced = travelling.astype(F32) + arriving.astype(F32) + term[0].astype(F32)
    reduced = reduced.astype(BF16)
    reduced = (reduced.astype(F32) + swap_chip(reduced).astype(F32)).astype(BF16)
    reduced, values, input_grad = lax.optimization_barrier((reduced, values, input_grad))
    other = swap_core(reduced)
    qkv_grad, out_grad = pl.pallas_call(
        finish_kernel,
        name="finish",
        out_shape=(
            jax.ShapeDtypeStruct((depth, 3 * width), F32),
            jax.ShapeDtypeStruct((depth, width), F32),
        ),
        in_specs=[smem_spec()] + [vmem_spec()] * 4,
        out_specs=[vmem_spec()] * 2,
        compiler_params=params(14),
        cost_estimate=cost(2),
    )(env_index, reduced, other, u, w_value[None])
    return values, input_grad[None, None], qkv_grad, out_grad


def solution(mesh):
    in_specs = (
        P("env", "tm", None, None),
        P("env", "tm"),
        P("env", None, "tm"),
        P("env", None, "tm"),
        P(),
        P(),
        P(),
        P(),
        P("tm", None),
        P("tm", None),
        P(),
    )
    out_specs = (P("env", None, "tm"), P("env", "tm", None, None), P("tm", None), P("tm", None))
    body = functools.partial(per_device, mesh.shape["env"], mesh.shape["tm"])
    return jax.shard_map(
        body, mesh=mesh, in_specs=in_specs, out_specs=out_specs, check_vma=False
    )
```

```python
import functools
import math

import jax
import jax.numpy as jnp
from jax import lax
from jax.experimental import pallas as pl
from jax.experimental.pallas import tpu as pltpu
from jax.sharding import PartitionSpec as P

HEADS = 8
EPS = 1e-06
F32 = jnp.float32
BF16 = jnp.bfloat16
TILE = 256


def dot_nn(a, b):
    return lax.dot_general(a, b, (((1,), (0,)), ((), ())), preferred_element_type=F32)


def dot_nt(a, b):
    return lax.dot_general(a, b, (((1,), (1,)), ((), ())), preferred_element_type=F32)


def dot_tn(a, b):
    return lax.dot_general(a, b, (((0,), (0,)), ((), ())), preferred_element_type=F32)


def inv_rms(rows):
    return lax.rsqrt(jnp.mean(rows * rows, axis=-1, keepdims=True) + EPS)


def norm_pull(rows, gain, grad):
    scale = inv_rms(rows)
    scaled = grad * gain
    inner = jnp.mean(scaled * rows, axis=-1, keepdims=True)
    return scale * scaled - rows * (scale * scale * scale * inner)


def spans(total, size):
    size = min(size, total)
    return [pl.ds(at, size) for at in range(0, total, size)]


def core_of(env_ref):
    return env_ref[0] % 2


def place_of(env_ref, tm_ref, count, hop):
    at = tm_ref[0]
    way = 1 - 2 * ((env_ref[0] + env_ref[0] // 2) % 2)
    spot = jnp.where(at % 2 == 0, at // 2, count - 1 - at // 2)
    spot = (spot + way * hop + count) % count
    return jnp.where(spot < count // 2, 2 * spot, 2 * (count - 1 - spot) + 1)


def copies_of(moves, sems):
    return [
        pltpu.make_async_copy(source, target, sems.at[at])
        for at, (source, target) in enumerate(moves)
    ]


def started(moves, sems):
    copies = copies_of(moves, sems)
    for copy in copies:
        copy.start()
    return copies


def temporal_forward(
    done_ref, rows_ref, gain_ref, w_qkv_hbm, w_out_hbm, h1_ref, qkv_hbm, probs_hbm,
    w_qkv, w_out, qkv_ref, probs_ref, mixed, sems, out_sems,
):
    length, width = rows_ref.shape
    size = width // HEADS
    chunks = spans(3 * width, width // 2)
    moves = [(w_qkv_hbm.at[:, span], w_qkv.at[:, span]) for span in chunks]
    copies = started(moves + [(w_out_hbm, w_out)], sems)
    rows = rows_ref[...].astype(F32)
    normed = (rows * inv_rms(rows) * gain_ref[...]).astype(BF16)
    outs = copies_of(
        [(qkv_ref, qkv_hbm)] + [(probs_ref.at[head], probs_hbm.at[head]) for head in range(HEADS)],
        out_sems,
    )
    for part, chunk in enumerate(chunks):
        copies[part].wait()
        for at in range(chunk.start, chunk.start + chunk.size, TILE):
            span = pl.ds(at, TILE)
            qkv_ref[:, span] = dot_nn(normed, w_qkv[:, span]).astype(BF16)
    outs[0].start()
    done = done_ref[0]
    query_at = lax.broadcasted_iota(jnp.int32, (length, length), 0)
    key_at = lax.broadcasted_iota(jnp.int32, (length, length), 1)
    allowed = (key_at <= query_at) & ((key_at > done) == (query_at > done))
    bias = jnp.where(allowed, 0.0, -1e30)
    for head in range(HEADS):
        queries = qkv_ref[:, pl.ds(head * size, size)]
        keys = qkv_ref[:, pl.ds(width + head * size, size)]
        values = qkv_ref[:, pl.ds(2 * width + head * size, size)]
        scores = dot_nt(queries, keys) * (1.0 / math.sqrt(size)) + bias
        weights = jnp.exp(scores - jnp.max(scores, axis=-1, keepdims=True))
        probs = weights * (1.0 / jnp.sum(weights, axis=-1, keepdims=True))
        probs = probs.astype(BF16)
        probs_ref[head] = probs
        outs[1 + head].start()
        mixed[:, pl.ds(head * size, size)] = dot_nn(probs, values).astype(BF16)
    copies[-1].wait()
    for span in spans(width, TILE):
        added = dot_nn(mixed[...], w_out[:, span])
        h1_ref[:, span] = (rows_ref[:, span].astype(F32) + added).astype(BF16)
    for out in outs:
        out.wait()


def mix_grad_kernel(
    first_head, grad_hbm, w_hbm, qkv_hbm, probs_hbm, out_ref, grad_ref, w_ref, qkv_ref, probs_ref,
    grad_mixed, sems,
):
    length, width = grad_ref.shape
    size = width // HEADS
    heads, part = probs_ref.shape[0], out_ref.shape[1] // 3
    scale = 1.0 / math.sqrt(size)
    tiles, start = part // TILE, first_head * size

    def w_copy(step):
        source = pl.ds(pl.multiple_of(start + step * TILE, TILE), TILE)
        target = pl.ds(pl.multiple_of(step * TILE, TILE), TILE)
        return pltpu.make_async_copy(w_hbm.at[source, :], w_ref.at[target, :], sems.at[step])

    grad_copy = pltpu.make_async_copy(grad_hbm, grad_ref, sems.at[tiles + 4])
    grad_copy.start()
    for step in range(tiles):
        w_copy(step).start()
    moves = [
        (qkv_hbm.at[:, pl.ds(at * width + start, part)], qkv_ref.at[:, pl.ds(at * part, part)])
        for at in range(3)
    ]
    moves.append((probs_hbm.at[pl.ds(first_head, heads)], probs_ref))
    copies = [
        pltpu.make_async_copy(source, target, sems.at[tiles + at])
        for at, (source, target) in enumerate(moves)
    ]
    for copy in copies:
        copy.start()
    grad_copy.wait()

    @pl.loop(0, tiles)
    def _(step):
        w_copy(step).wait()
        span = pl.ds(pl.multiple_of(step * TILE, TILE), TILE)
        grad_mixed[:, span] = dot_nt(grad_ref[...], w_ref[span, :]).astype(BF16)

    for copy in copies:
        copy.wait()
    for head in range(heads):
        query_span = pl.ds(head * size, size)
        key_span = pl.ds(part + head * size, size)
        value_span = pl.ds(2 * part + head * size, size)
        probs = probs_ref[head]
        head_grad = grad_mixed[:, query_span]
        out_ref[:, value_span] = dot_tn(probs, head_grad).astype(BF16)
        grad_probs = dot_nt(head_grad, qkv_ref[:, value_span])
        wide = probs.astype(F32)
        inner = jnp.sum(wide * grad_probs, axis=-1, keepdims=True)
        grad_scores = (wide * (grad_probs - inner) * scale).astype(BF16)
        out_ref[:, query_span] = dot_nn(grad_scores, qkv_ref[:, key_span]).astype(BF16)
        out_ref[:, key_span] = dot_tn(grad_scores, qkv_ref[:, query_span]).astype(BF16)


def norm_grad_kernel(
    gain_ref, grad_hbm, rows_hbm, low_hbm, high_hbm, w_hbm, out_ref,
    grad_ref, rows_ref, low_ref, high_ref, w_ref, grad_normed, sems,
):
    width = rows_ref.shape[1]
    tiles, part = width // TILE, low_ref.shape[1] // 3

    def rows_of(step):
        return pl.ds(pl.multiple_of(step * TILE, TILE), TILE)

    def w_copy(step):
        return pltpu.make_async_copy(
            w_hbm.at[rows_of(step), :], w_ref.at[rows_of(step), :], sems.at[step]
        )

    moves = [(low_hbm, low_ref), (high_hbm, high_ref), (grad_hbm, grad_ref), (rows_hbm, rows_ref)]
    copies = [
        pltpu.make_async_copy(source, target, sems.at[tiles + at])
        for at, (source, target) in enumerate(moves)
    ]
    for copy in copies[:2]:
        copy.start()
    for step in range(tiles):
        w_copy(step).start()
    for copy in copies[2:]:
        copy.start()
    for copy in copies[:2]:
        copy.wait()

    @pl.loop(0, tiles)
    def _(step):
        w_copy(step).wait()
        total = None
        for side, grads_ref in enumerate((low_ref, high_ref)):
            for at in range(3):
                columns = pl.ds(at * width + side * part, part)
                product = dot_nt(grads_ref[:, pl.ds(at * part, part)], w_ref[rows_of(step), columns])
                total = product if total is None else total + product
        grad_normed[:, rows_of(step)] = total

    for copy in copies[2:]:
        copy.wait()
    rows = rows_ref[...].astype(F32)
    pulled = norm_pull(rows, gain_ref[...], grad_normed[...])
    out_ref[...] = (grad_ref[...].astype(F32) + pulled).astype(BF16)


def agent_kernel(
    blocks, group_steps, env_ref, tm_ref, rows_ref, alive_ref, target_ref, gain_ref, value_ref,
    shard_ref, own_ref, *rest,
):
    moved = rest[: 2 * blocks]
    grad_ref, pack_ref, keep_ref, extra_ref, u_ref, predicted_ref = rest[2 * blocks : 2 * blocks + 6]
    w_all, qk, grad_qk, probs_all, slopes, column, grad_normed, sems = rest[2 * blocks + 6 :]
    total_rows, width = rows_ref.shape
    size = width // HEADS
    scale = 1.0 / math.sqrt(size)
    normed_ref = pack_ref.at[pl.ds(0, total_rows), :]
    groups, group_rows = alive_ref.shape[0], alive_ref.shape[2]
    agents = group_rows // group_steps
    local_steps = total_rows // agents
    depth, block_width = own_ref.shape
    middle = width // 2
    w_q, w_k = w_all.at[:, pl.ds(0, width)], w_all.at[:, pl.ds(block_width, width)]
    w_v = [
        w_all.at[:, pl.ds(width, middle)],
        w_all.at[:, pl.ds(block_width + width, middle)],
    ]
    core = core_of(env_ref)
    other = 1 - core
    near = blocks // 2
    far = blocks - near
    own_hops = [-hop for hop in range(1, far + 1)] + list(range(1, near + 1))
    hops = own_hops + [-hop for hop in own_hops]

    def row_span(hop):
        place = place_of(env_ref, tm_ref, blocks + 1, hop)
        return pl.ds(pl.multiple_of(place * depth, depth), depth)

    def column_span(start, length):
        return pl.ds(pl.multiple_of(start, 128), length)

    own_rows = row_span(0)
    other_at = other * block_width
    moves = [
        (own_ref, w_all.at[own_rows, column_span(core * block_width, block_width)]),
        (
            own_ref.at[:, pl.ds(block_width - 128, 128)],
            w_all.at[own_rows, column_span(other_at + block_width - 128, 128)],
        ),
        (
            shard_ref.at[:, column_span(other * width, width)],
            w_all.at[own_rows, column_span(other_at, width)],
        ),
        (
            shard_ref.at[:, column_span(2 * width + other * middle, middle)],
            w_all.at[own_rows, column_span(other_at + width, middle)],
        ),
    ]
    for at in range(2 * blocks):
        half = core if at < blocks else other
        moves.append(
            (moved[at], w_all.at[row_span(hops[at]), column_span(half * block_width, block_width)])
        )
    copies = started(moves, sems)

    def row_spans(group):
        if groups == 1:
            return [(pl.ds(0, total_rows), pl.ds(0, total_rows))]
        return [
            (
                pl.ds(agent * local_steps + group * group_steps, group_steps),
                pl.ds(group * group_rows + agent * group_steps, group_steps),
            )
            for agent in range(agents)
        ]

    def to_column(row):
        return jnp.transpose(jnp.broadcast_to(row, (128, row.shape[1])))[:, :1]

    for group in range(groups):
        for source, target in row_spans(group):
            rows = rows_ref[source, :].astype(F32)
            normed_ref[target, :] = (rows * inv_rms(rows) * gain_ref[...]).astype(BF16)
            column[target, :] = jnp.broadcast_to(
                jnp.sum(rows * value_ref[...], axis=-1, keepdims=True), (rows.shape[0], 128)
            )
    for copy in copies:
        copy.wait()

    u_parts = jnp.transpose(w_all[:, pl.ds(block_width - 128, 128)].astype(F32))
    u_high, u_low = u_parts[0:1], u_parts[1:2]
    u_ref[...] = u_high + u_low
    part_at = lax.broadcasted_iota(jnp.int32, (2 * HEADS, width), 0)
    head_at = lax.broadcasted_iota(jnp.int32, (2 * HEADS, width), 1) // size
    by_head = jnp.where(
        head_at == part_at % HEADS, jnp.where(part_at < HEADS, u_high, u_low), 0.0
    ).astype(BF16)
    both = dot_nt(by_head[:, :middle], w_v[0][...]) + dot_nt(by_head[:, middle:], w_v[1][...])
    folded = both[:HEADS] + both[HEADS:]
    folded_high = folded.astype(BF16)
    folded_parts = jnp.concatenate(
        [folded_high.astype(F32), folded - folded_high.astype(F32)], axis=0
    ).astype(BF16)
    both = dot_nt(folded_parts, normed_ref[...])
    folded_rows = both[:HEADS] + both[HEADS:]
    for at in range(0, width, TILE):
        qk[:, pl.ds(at, TILE)] = dot_nn(normed_ref[...], w_q[:, pl.ds(at, TILE)]).astype(BF16)
    for at in range(0, width, TILE):
        qk[:, pl.ds(width + at, TILE)] = dot_nn(
            normed_ref[...], w_k[:, pl.ds(at, TILE)]
        ).astype(BF16)

    row_at = lax.broadcasted_iota(jnp.int32, (group_rows, group_rows), 0)
    col_at = lax.broadcasted_iota(jnp.int32, (group_rows, group_rows), 1)
    same_step = row_at % group_steps == col_at % group_steps
    pulls = []
    for group in range(groups):
        group_span = pl.ds(group * group_rows, group_rows)
        alive = alive_ref[group]
        allowed = same_step & ((alive > 0.5) | (row_at == col_at))
        bias = jnp.where(allowed, 0.0, -1e30)
        predicted = column[group_span, :1]
        for head in range(HEADS):
            queries = qk[group_span, pl.ds(head * size, size)]
            keys = qk[group_span, pl.ds(width + head * size, size)]
            scores = dot_nt(queries, keys) * scale + bias
            weights = jnp.exp(scores - jnp.max(scores, axis=-1, keepdims=True))
            probs = weights * (1.0 / jnp.sum(weights, axis=-1, keepdims=True))
            weighted = probs * folded_rows[
                head : head + 1, group * group_rows : (group + 1) * group_rows
            ]
            pooled = jnp.sum(weighted, axis=-1, keepdims=True)
            predicted = predicted + pooled
            probs_all[group * HEADS + head] = probs
            slopes[group * HEADS + head] = (weighted - probs * pooled) * scale
        error = 32.0 * to_column(alive) * (predicted - to_column(target_ref[group]))
        predicted_ref[group] = jnp.transpose(jnp.broadcast_to(predicted, (group_rows, 128)))[:8]
        column[group_span, :] = jnp.broadcast_to(error, (group_rows, 128))
        pull_rows = []
        for head in range(HEADS):
            query_span = pl.ds(head * size, size)
            key_span = pl.ds(width + head * size, size)
            grad_scores = (slopes[group * HEADS + head] * error).astype(BF16)
            grad_qk[group_span, query_span] = dot_nn(
                grad_scores, qk[group_span, key_span]
            ).astype(BF16)
            grad_qk[group_span, key_span] = dot_tn(
                grad_scores, qk[group_span, query_span]
            ).astype(BF16)
            pull_rows.append(
                jnp.sum(probs_all[group * HEADS + head] * error, axis=0, keepdims=True)
            )
        pulls.append(jnp.concatenate(pull_rows, axis=0))
    pull = jnp.concatenate(pulls, axis=1) if groups > 1 else pulls[0]
    pull = pull.astype(BF16)
    twice = jnp.concatenate([pull, pull], axis=0)
    for at in range(0, width, TILE):
        span = pl.ds(at, TILE)
        grad_normed[:, span] = (
            dot_nt(grad_qk[:, pl.ds(0, width)], w_q[span, :])
            + dot_nt(grad_qk[:, pl.ds(width, width)], w_k[span, :])
            + dot_tn(twice, folded_parts[:, at : at + TILE])
        )
    for group in range(groups):
        for source, target in row_spans(group):
            rows = rows_ref[source, :].astype(F32)
            pulled = norm_pull(rows, gain_ref[...], grad_normed[target, :])
            top = column[target, :1] * value_ref[...]
            grad_ref[source, :] = (top + pulled).astype(BF16)
    keep_ref[...] = grad_qk[:, column_span(core * width, width)]
    pack_ref[pl.ds(total_rows, total_rows), :] = grad_qk[:, column_span(other * width, width)]

    folded_grad = dot_nn(pull, normed_ref[...])
    folded_grad_low = folded_grad.astype(BF16)
    pooled = jnp.concatenate(
        [dot_nn(folded_grad_low, w_v[0][...]), dot_nn(folded_grad_low, w_v[1][...])], axis=1
    )
    pooled = jnp.sum(
        jnp.where(head_at[:HEADS] == part_at[:HEADS], pooled, 0.0), axis=0, keepdims=True
    )
    extra = jnp.concatenate(
        [folded_grad, pooled, jnp.zeros((127 - HEADS, width), F32)], axis=0
    )
    extra_ref[...] = jnp.transpose(extra).astype(BF16)


def weight_grad_kernel(hops, env_ref, tm_ref, pack_ref, keep_ref, moved_ref, extra_ref, *rest):
    outs, (total, sems) = rest[:-2], rest[-2:]
    half, width = keep_ref.shape
    depth = width // len(outs)
    own, other = pl.ds(0, half), pl.ds(half, half)
    total[:, pl.ds(width, 128)] = extra_ref[...]
    for rows in spans(width, TILE):
        for columns in spans(width, TILE):
            total[rows, columns] = (
                dot_tn(pack_ref[own, rows], keep_ref[:, columns])
                + dot_tn(moved_ref[own, rows], moved_ref[other, columns])
            ).astype(BF16)
    copies = [
        pltpu.make_async_copy(
            total.at[
                pl.ds(
                    pl.multiple_of(place_of(env_ref, tm_ref, len(outs), hop) * depth, depth), depth
                ),
                :,
            ],
            out,
            sems.at[at],
        )
        for at, (hop, out) in enumerate(zip(hops, outs))
    ]
    for copy in copies:
        copy.start()
    for copy in copies:
        copy.wait()


def pack_block_kernel(env_ref, qk_ref, v_ref, w_out_ref, value_ref, out_ref):
    width, middle = qk_ref.shape[1], v_ref.shape[1]
    out_ref[:, pl.ds(0, width)] = qk_ref[...]
    out_ref[:, pl.ds(width, middle)] = v_ref[...]
    u = jnp.sum(w_out_ref[...].astype(F32) * value_ref[...], axis=-1, keepdims=True)
    high = u.astype(BF16).astype(F32)
    lane = lax.broadcasted_iota(jnp.int32, (qk_ref.shape[0], 128), 1)
    parts = jnp.where(lane == 0, high, jnp.where(lane == 1, u - high, 0.0))
    out_ref[:, pl.ds(width + middle, 128)] = parts.astype(BF16)


def finish_kernel(env_ref, own_ref, other_ref, u_ref, value_ref, qkv_ref, out_ref):
    width = u_ref.shape[1]
    size = width // HEADS
    own, other = own_ref[:, pl.ds(0, width)], other_ref[:, pl.ds(0, width)]
    core = core_of(env_ref)
    qkv_ref[:, pl.ds(pl.multiple_of(core * width, width), width)] = own.astype(F32)
    qkv_ref[:, pl.ds(pl.multiple_of((1 - core) * width, width), width)] = other.astype(F32)
    extra = own_ref[:, pl.ds(width, 128)].astype(F32) + other_ref[:, pl.ds(width, 128)].astype(F32)
    for head in range(HEADS):
        qkv_ref[:, pl.ds(2 * width + head * size, size)] = (
            extra[:, head : head + 1] * u_ref[:, pl.ds(head * size, size)]
        )
    out_ref[...] = extra[:, HEADS : HEADS + 1] * value_ref[...]


def any_spec():
    return pl.BlockSpec(memory_space=pl.ANY)


def hbm_spec():
    return pl.BlockSpec(memory_space=pltpu.HBM)


def vmem_spec():
    return pl.BlockSpec(memory_space=pltpu.VMEM)


def smem_spec():
    return pl.BlockSpec(memory_space=pltpu.SMEM)


def params(mebibytes=60):
    return pltpu.CompilerParams(vmem_limit_bytes=mebibytes * 1024 * 1024)


def cost(microseconds):
    return pl.CostEstimate(
        flops=int(microseconds * 1e9), bytes_accessed=int(microseconds * 2e6), transcendentals=0
    )


def ring_order(count):
    return list(range(0, count, 2)) + list(range(count - 1, 0, -2))


def per_device(
    env_count, tm_count,
    hidden, done_step, alive, targets, gain_t, w_qkv_t, w_out_t, gain_a, w_qkv_a, w_out_a, w_value,
):
    length, width = hidden.shape[2:]
    agents, local_steps = alive.shape[1:]
    depth = w_qkv_a.shape[0]
    env_index = lax.axis_index("env").astype(jnp.int32)[None]
    tm_index = lax.axis_index("tm").astype(jnp.int32)[None]
    order = ring_order(tm_count)
    spot = [order.index(at) for at in range(tm_count)]

    ways = [1 if at in (0, 3) else -1 for at in range(env_count)]

    def ring(block, along=1):
        pairs = [
            (env * tm_count + at, env * tm_count + order[(spot[at] + along * ways[env]) % tm_count])
            for env in range(env_count)
            for at in range(tm_count)
        ]
        return lax.ppermute(block, ("env", "tm"), pairs)

    def ring_other_chip(block):
        pairs = [
            (env * tm_count + at, (env ^ 2) * tm_count + order[(spot[at] + ways[env]) % tm_count])
            for env in range(env_count)
            for at in range(tm_count)
        ]
        return lax.ppermute(block, ("env", "tm"), pairs)

    def swap_core(block):
        return lax.ppermute(block, "env", [(at, at ^ 1) for at in range(env_count)])

    def swap_chip(block):
        return lax.ppermute(block, "env", [(at, at ^ 2) for at in range(env_count)])

    far = tm_count // 2
    near = tm_count - 1 - far

    block_width = width + width // 2 + 128
    own_block = pl.pallas_call(
        pack_block_kernel,
        name="pack_block",
        out_shape=jax.ShapeDtypeStruct((depth, block_width), BF16),
        grid_spec=pltpu.PrefetchScalarGridSpec(
            num_scalar_prefetch=1,
            grid=(1,),
            in_specs=[
                pl.BlockSpec((depth, width), lambda at, env: (0, core_of(env))),
                pl.BlockSpec((depth, width // 2), lambda at, env: (0, 4 + core_of(env))),
                pl.BlockSpec((depth, width), lambda at, env: (0, 0)),
                pl.BlockSpec((1, width), lambda at, env: (0, 0)),
            ],
            out_specs=pl.BlockSpec((depth, block_width), lambda at, env: (0, 0)),
        ),
        compiler_params=params(),
        cost_estimate=cost(2),
    )(env_index, w_qkv_a, w_qkv_a, w_out_a, w_value[None])
    first_block = ring(own_block)

    rows = hidden[0, 0]
    h1, qkv, probs = pl.pallas_call(
        temporal_forward,
        name="temporal_forward",
        out_shape=(
            jax.ShapeDtypeStruct((length, width), BF16),
            jax.ShapeDtypeStruct((length, 3 * width), BF16),
            jax.ShapeDtypeStruct((HEADS, length, length), BF16),
        ),
        in_specs=[smem_spec()] + [vmem_spec()] * 2 + [hbm_spec()] * 2,
        out_specs=[vmem_spec()] + [hbm_spec()] * 2,
        scratch_shapes=[
            pltpu.VMEM((width, 3 * width), BF16),
            pltpu.VMEM((width, width), BF16),
            pltpu.VMEM((length, 3 * width), BF16),
            pltpu.VMEM((HEADS, length, length), BF16),
            pltpu.VMEM((length, width), BF16),
            pltpu.SemaphoreType.DMA((7,)),
            pltpu.SemaphoreType.DMA((HEADS + 1,)),
        ],
        compiler_params=params(),
        cost_estimate=cost(8),
    )(done_step[0], rows, gain_t[None], w_qkv_t, w_out_t)
    h1, first_block = lax.optimization_barrier((h1, first_block))
    lifted = lax.all_to_all(h1, "tm", split_axis=0, concat_axis=0, tiled=True)

    ringed, crossed = [first_block], []
    for hop in range(1, far):
        if len(crossed) > 0:
            ringed[-1], crossed[-1] = lax.optimization_barrier((ringed[-1], crossed[-1]))
        if hop <= near:
            crossed.append(swap_chip(ringed[-1]))
        ringed.append(ring(ringed[-1]))
    crossed += [swap_chip(block) for block in ringed[len(crossed) : near]]
    own_blocks = ringed + crossed
    gated = far + near // 2
    lifted, own_blocks[gated] = lax.optimization_barrier((lifted, own_blocks[gated]))
    other_blocks = [swap_core(block) for block in own_blocks]

    group_steps = 16 if local_steps % 16 == 0 else local_steps
    groups = local_steps // group_steps
    group_rows = agents * group_steps

    def grouped(block):
        block = block.reshape(agents, groups, group_steps)
        return jnp.swapaxes(block, 0, 1).reshape(groups, 1, group_rows)

    total_rows = agents * local_steps
    grad_lifted, pack, keep, extra, u, predicted = pl.pallas_call(
        functools.partial(agent_kernel, tm_count - 1, group_steps),
        name="agent_block",
        out_shape=(
            jax.ShapeDtypeStruct((total_rows, width), BF16),
            jax.ShapeDtypeStruct((2 * total_rows, width), BF16),
            jax.ShapeDtypeStruct((total_rows, width), BF16),
            jax.ShapeDtypeStruct((width, 128), BF16),
            jax.ShapeDtypeStruct((1, width), F32),
            jax.ShapeDtypeStruct((groups, 8, group_rows), F32),
        ),
        in_specs=[smem_spec()] * 2 + [vmem_spec()] * 5 + [hbm_spec()] * (2 * tm_count),
        out_specs=[vmem_spec()] * 6,
        scratch_shapes=[
            pltpu.VMEM((width, 2 * block_width), BF16),
            pltpu.VMEM((total_rows, 2 * width), BF16),
            pltpu.VMEM((total_rows, 2 * width), BF16),
            pltpu.VMEM((groups * HEADS, group_rows, group_rows), F32),
            pltpu.VMEM((groups * HEADS, group_rows, group_rows), F32),
            pltpu.VMEM((total_rows, 128), F32),
            pltpu.VMEM((total_rows, width), F32),
            pltpu.SemaphoreType.DMA((2 * tm_count + 2,)),
        ],
        compiler_params=params(),
        cost_estimate=cost(11),
    )(
        env_index, tm_index, lifted, grouped(alive[0].astype(F32)), grouped(targets[0]), gain_a[None],
        w_value[None], w_qkv_a, own_block, *own_blocks, *other_blocks,
    )
    values = predicted[:, 0].reshape(groups, agents, group_steps)
    values = jnp.swapaxes(values, 0, 1).reshape(1, agents, local_steps)

    returned = lax.all_to_all(grad_lifted, "tm", split_axis=0, concat_axis=0, tiled=True)

    moved = swap_core(pack)
    hops = list(range(far + 1)) + [-hop for hop in range(1, near + 1)]
    terms = pl.pallas_call(
        functools.partial(weight_grad_kernel, hops),
        name="weight_grad",
        out_shape=[jax.ShapeDtypeStruct((depth, width + 128), BF16)] * tm_count,
        in_specs=[smem_spec()] * 2 + [vmem_spec()] * 4,
        out_specs=[any_spec()] * tm_count,
        scratch_shapes=[
            pltpu.VMEM((width, width + 128), BF16),
            pltpu.SemaphoreType.DMA((tm_count,)),
        ],
        compiler_params=params(20),
        cost_estimate=cost(4),
    )(env_index, tm_index, pack, keep, moved, extra)
    def mix_grad(first_head):
        heads, part = HEADS // 2, width // 2
        return pl.pallas_call(
            functools.partial(mix_grad_kernel, first_head),
            name="temporal_mix_grad",
            out_shape=jax.ShapeDtypeStruct((length, 3 * part), BF16),
            in_specs=[hbm_spec()] * 4,
            out_specs=vmem_spec(),
            scratch_shapes=[
                pltpu.VMEM((length, width), BF16),
                pltpu.VMEM((part, width), BF16),
                pltpu.VMEM((length, 3 * part), BF16),
                pltpu.VMEM((heads, length, length), BF16),
                pltpu.VMEM((length, part), BF16),
                pltpu.SemaphoreType.DMA((part // TILE + 5,)),
            ],
            compiler_params=params(),
            cost_estimate=cost(4),
        )(returned, w_out_t, qkv, probs)

    term = dict(zip(hops, terms))
    travelling = ring(term[far])
    chip_terms = {hop: swap_chip(term[-hop]) for hop in range(near, 1, -1)}
    arriving = ring(term[-1], -1)
    for hop in range(far - 1, 0, -1):
        if hop == far - 1:
            travelling, returned, arriving = lax.optimization_barrier(
                (travelling, returned, arriving)
            )
            near_sum = (arriving.astype(F32) + term[0].astype(F32)).astype(BF16)
            far_sum = swap_chip(near_sum)
        if hop == max(far - 2, 1):
            travelling, low_grads = lax.optimization_barrier((travelling, mix_grad(0)))
        if hop == max(far - 3, 1):
            travelling, high_grads, far_sum = lax.optimization_barrier(
                (travelling, mix_grad(HEADS // 2), far_sum)
            )
        total = travelling.astype(F32) + term[hop].astype(F32)
        if hop in chip_terms:
            total = total + chip_terms[hop].astype(F32)
        total = total.astype(BF16)
        if hop == 1:
            crossing = ring_other_chip(total)
        travelling = ring(total)
    input_grad = pl.pallas_call(
        norm_grad_kernel,
        name="temporal_norm_grad",
        out_shape=jax.ShapeDtypeStruct((length, width), BF16),
        in_specs=[vmem_spec()] + [hbm_spec()] * 5,
        out_specs=vmem_spec(),
        scratch_shapes=[
            pltpu.VMEM((length, width), BF16),
            pltpu.VMEM((length, width), BF16),
            pltpu.VMEM((length, 3 * width // 2), BF16),
            pltpu.VMEM((length, 3 * width // 2), BF16),
            pltpu.VMEM((width, 3 * width), BF16),
            pltpu.VMEM((length, width), F32),
            pltpu.SemaphoreType.DMA((width // TILE + 4,)),
        ],
        compiler_params=params(),
        cost_estimate=cost(6),
    )(gain_t[None], returned, rows, low_grads, high_grads, w_qkv_t)
    reduced = travelling.astype(F32) + crossing.astype(F32)
    reduced = (reduced + near_sum.astype(F32) + far_sum.astype(F32)).astype(BF16)
    reduced, values, input_grad = lax.optimization_barrier((reduced, values, input_grad))
    other = swap_core(reduced)
    qkv_grad, out_grad = pl.pallas_call(
        finish_kernel,
        name="finish",
        out_shape=(
            jax.ShapeDtypeStruct((depth, 3 * width), F32),
            jax.ShapeDtypeStruct((depth, width), F32),
        ),
        in_specs=[smem_spec()] + [vmem_spec()] * 4,
        out_specs=[vmem_spec()] * 2,
        compiler_params=params(14),
        cost_estimate=cost(2),
    )(env_index, reduced, other, u, w_value[None])
    return values, input_grad[None, None], qkv_grad, out_grad


def solution(mesh):
    in_specs = (
        P("env", "tm", None, None),
        P("env", "tm"),
        P("env", None, "tm"),
        P("env", None, "tm"),
        P(),
        P(),
        P(),
        P(),
        P("tm", None),
        P("tm", None),
        P(),
    )
    out_specs = (P("env", None, "tm"), P("env", "tm", None, None), P("tm", None), P("tm", None))
    body = functools.partial(per_device, mesh.shape["env"], mesh.shape["tm"])
    return jax.shard_map(
        body, mesh=mesh, in_specs=in_specs, out_specs=out_specs, check_vma=False
    )
```

```python
import functools
import math

import jax
import jax.numpy as jnp
from jax import lax
from jax.experimental import pallas as pl
from jax.experimental.pallas import tpu as pltpu
from jax.sharding import PartitionSpec as P

HEADS = 8
EPS = 1e-06
F32 = jnp.float32
BF16 = jnp.bfloat16
TILE = 256


def dot_nn(a, b):
    return lax.dot_general(a, b, (((1,), (0,)), ((), ())), preferred_element_type=F32)


def dot_nt(a, b):
    return lax.dot_general(a, b, (((1,), (1,)), ((), ())), preferred_element_type=F32)


def dot_tn(a, b):
    return lax.dot_general(a, b, (((0,), (0,)), ((), ())), preferred_element_type=F32)


def inv_rms(rows):
    return lax.rsqrt(jnp.mean(rows * rows, axis=-1, keepdims=True) + EPS)


def norm_pull(rows, gain, grad):
    scale = inv_rms(rows)
    scaled = grad * gain
    inner = jnp.mean(scaled * rows, axis=-1, keepdims=True)
    return scale * scaled - rows * (scale * scale * scale * inner)


def spans(total, size):
    size = min(size, total)
    return [pl.ds(at, size) for at in range(0, total, size)]


def core_of(env_ref):
    return env_ref[0] % 2


def place_of(env_ref, tm_ref, count, hop):
    at = tm_ref[0]
    way = 1 - 2 * ((env_ref[0] + env_ref[0] // 2) % 2)
    spot = jnp.where(at % 2 == 0, at // 2, count - 1 - at // 2)
    spot = (spot + way * hop + count) % count
    return jnp.where(spot < count // 2, 2 * spot, 2 * (count - 1 - spot) + 1)


def copies_of(moves, sems):
    return [
        pltpu.make_async_copy(source, target, sems.at[at])
        for at, (source, target) in enumerate(moves)
    ]


def started(moves, sems):
    copies = copies_of(moves, sems)
    for copy in copies:
        copy.start()
    return copies


def temporal_forward(
    done_ref, rows_ref, gain_ref, w_qkv_hbm, w_out_hbm, h1_ref, qkv_hbm, probs_hbm,
    w_qkv, w_out, qkv_ref, probs_ref, mixed, sems, out_sems,
):
    length, width = rows_ref.shape
    size = width // HEADS
    chunks = spans(3 * width, width // 2)
    moves = [(w_qkv_hbm.at[:, span], w_qkv.at[:, span]) for span in chunks]
    copies = started(moves + [(w_out_hbm, w_out)], sems)
    rows = rows_ref[...].astype(F32)
    normed = (rows * inv_rms(rows) * gain_ref[...]).astype(BF16)
    outs = copies_of(
        [(qkv_ref, qkv_hbm)] + [(probs_ref.at[head], probs_hbm.at[head]) for head in range(HEADS)],
        out_sems,
    )
    for part, chunk in enumerate(chunks):
        copies[part].wait()
        for at in range(chunk.start, chunk.start + chunk.size, TILE):
            span = pl.ds(at, TILE)
            qkv_ref[:, span] = dot_nn(normed, w_qkv[:, span]).astype(BF16)
    outs[0].start()
    done = done_ref[0]
    query_at = lax.broadcasted_iota(jnp.int32, (length, length), 0)
    key_at = lax.broadcasted_iota(jnp.int32, (length, length), 1)
    allowed = (key_at <= query_at) & ((key_at > done) == (query_at > done))
    bias = jnp.where(allowed, 0.0, -1e30)
    for head in range(HEADS):
        queries = qkv_ref[:, pl.ds(head * size, size)]
        keys = qkv_ref[:, pl.ds(width + head * size, size)]
        values = qkv_ref[:, pl.ds(2 * width + head * size, size)]
        scores = dot_nt(queries, keys) * (1.0 / math.sqrt(size)) + bias
        weights = jnp.exp(scores - jnp.max(scores, axis=-1, keepdims=True))
        probs = weights * (1.0 / jnp.sum(weights, axis=-1, keepdims=True))
        probs = probs.astype(BF16)
        probs_ref[head] = probs
        outs[1 + head].start()
        mixed[:, pl.ds(head * size, size)] = dot_nn(probs, values).astype(BF16)
    copies[-1].wait()
    for span in spans(width, TILE):
        added = dot_nn(mixed[...], w_out[:, span])
        h1_ref[:, span] = (rows_ref[:, span].astype(F32) + added).astype(BF16)
    for out in outs:
        out.wait()


def mix_grad_kernel(
    first_head, grad_hbm, w_hbm, qkv_hbm, probs_hbm, out_ref, grad_ref, w_ref, qkv_ref, probs_ref,
    grad_mixed, sems,
):
    length, width = grad_ref.shape
    size = width // HEADS
    heads, part = probs_ref.shape[0], out_ref.shape[1] // 3
    scale = 1.0 / math.sqrt(size)
    tiles, start = part // TILE, first_head * size

    def w_copy(step):
        source = pl.ds(pl.multiple_of(start + step * TILE, TILE), TILE)
        target = pl.ds(pl.multiple_of(step * TILE, TILE), TILE)
        return pltpu.make_async_copy(w_hbm.at[source, :], w_ref.at[target, :], sems.at[step])

    grad_copy = pltpu.make_async_copy(grad_hbm, grad_ref, sems.at[tiles + 4])
    grad_copy.start()
    for step in range(tiles):
        w_copy(step).start()
    moves = [
        (qkv_hbm.at[:, pl.ds(at * width + start, part)], qkv_ref.at[:, pl.ds(at * part, part)])
        for at in range(3)
    ]
    moves.append((probs_hbm.at[pl.ds(first_head, heads)], probs_ref))
    copies = [
        pltpu.make_async_copy(source, target, sems.at[tiles + at])
        for at, (source, target) in enumerate(moves)
    ]
    for copy in copies:
        copy.start()
    grad_copy.wait()

    @pl.loop(0, tiles)
    def _(step):
        w_copy(step).wait()
        span = pl.ds(pl.multiple_of(step * TILE, TILE), TILE)
        grad_mixed[:, span] = dot_nt(grad_ref[...], w_ref[span, :]).astype(BF16)

    for copy in copies:
        copy.wait()
    for head in range(heads):
        query_span = pl.ds(head * size, size)
        key_span = pl.ds(part + head * size, size)
        value_span = pl.ds(2 * part + head * size, size)
        probs = probs_ref[head]
        head_grad = grad_mixed[:, query_span]
        out_ref[:, value_span] = dot_tn(probs, head_grad).astype(BF16)
        grad_probs = dot_nt(head_grad, qkv_ref[:, value_span])
        wide = probs.astype(F32)
        inner = jnp.sum(wide * grad_probs, axis=-1, keepdims=True)
        grad_scores = (wide * (grad_probs - inner) * scale).astype(BF16)
        out_ref[:, query_span] = dot_nn(grad_scores, qkv_ref[:, key_span]).astype(BF16)
        out_ref[:, key_span] = dot_tn(grad_scores, qkv_ref[:, query_span]).astype(BF16)


def norm_grad_kernel(
    gain_ref, grad_hbm, rows_hbm, low_hbm, high_hbm, w_hbm, out_ref,
    grad_ref, rows_ref, low_ref, high_ref, w_ref, grad_normed, sems,
):
    width = rows_ref.shape[1]
    tiles, part = width // TILE, low_ref.shape[1] // 3

    def rows_of(step):
        return pl.ds(pl.multiple_of(step * TILE, TILE), TILE)

    def w_copy(step):
        return pltpu.make_async_copy(
            w_hbm.at[rows_of(step), :], w_ref.at[rows_of(step), :], sems.at[step]
        )

    moves = [(low_hbm, low_ref), (high_hbm, high_ref), (grad_hbm, grad_ref), (rows_hbm, rows_ref)]
    copies = [
        pltpu.make_async_copy(source, target, sems.at[tiles + at])
        for at, (source, target) in enumerate(moves)
    ]
    for copy in copies[:2]:
        copy.start()
    for step in range(tiles):
        w_copy(step).start()
    for copy in copies[2:]:
        copy.start()
    for copy in copies[:2]:
        copy.wait()

    @pl.loop(0, tiles)
    def _(step):
        w_copy(step).wait()
        total = None
        for side, grads_ref in enumerate((low_ref, high_ref)):
            for at in range(3):
                columns = pl.ds(at * width + side * part, part)
                product = dot_nt(grads_ref[:, pl.ds(at * part, part)], w_ref[rows_of(step), columns])
                total = product if total is None else total + product
        grad_normed[:, rows_of(step)] = total

    for copy in copies[2:]:
        copy.wait()
    rows = rows_ref[...].astype(F32)
    pulled = norm_pull(rows, gain_ref[...], grad_normed[...])
    out_ref[...] = (grad_ref[...].astype(F32) + pulled).astype(BF16)


def agent_kernel(
    blocks, group_steps, env_ref, tm_ref, rows_ref, alive_ref, target_ref, gain_ref, value_ref,
    shard_ref, own_ref, *rest,
):
    moved = rest[: 2 * blocks]
    grad_ref, pack_ref, keep_ref, extra_ref, u_ref, predicted_ref = rest[2 * blocks : 2 * blocks + 6]
    w_all, qk, grad_qk, probs_all, slopes, column, grad_normed, normed_ref, sems, out_sems = rest[2 * blocks + 6 :]
    total_rows, width = rows_ref.shape
    size = width // HEADS
    scale = 1.0 / math.sqrt(size)
    groups, group_rows = alive_ref.shape[0], alive_ref.shape[2]
    agents = group_rows // group_steps
    local_steps = total_rows // agents
    depth, block_width = own_ref.shape
    middle = width // 2
    w_q, w_k = w_all.at[:, pl.ds(0, width)], w_all.at[:, pl.ds(block_width, width)]
    w_v = [
        w_all.at[:, pl.ds(width, middle)],
        w_all.at[:, pl.ds(block_width + width, middle)],
    ]
    core = core_of(env_ref)
    other = 1 - core
    near = blocks // 2
    far = blocks - near
    own_hops = [-hop for hop in range(1, far + 1)] + list(range(1, near + 1))
    hops = own_hops + [-hop for hop in own_hops]

    def row_span(hop):
        place = place_of(env_ref, tm_ref, blocks + 1, hop)
        return pl.ds(pl.multiple_of(place * depth, depth), depth)

    def column_span(start, length):
        return pl.ds(pl.multiple_of(start, 128), length)

    own_rows = row_span(0)
    other_at = other * block_width
    moves = [
        (own_ref, w_all.at[own_rows, column_span(core * block_width, block_width)]),
        (
            own_ref.at[:, pl.ds(block_width - 128, 128)],
            w_all.at[own_rows, column_span(other_at + block_width - 128, 128)],
        ),
        (
            shard_ref.at[:, column_span(other * width, width)],
            w_all.at[own_rows, column_span(other_at, width)],
        ),
        (
            shard_ref.at[:, column_span(2 * width + other * middle, middle)],
            w_all.at[own_rows, column_span(other_at + width, middle)],
        ),
    ]
    for at in range(2 * blocks):
        half = core if at < blocks else other
        moves.append(
            (moved[at], w_all.at[row_span(hops[at]), column_span(half * block_width, block_width)])
        )
    copies = started(moves, sems)

    def row_spans(group):
        if groups == 1:
            return [(pl.ds(0, total_rows), pl.ds(0, total_rows))]
        return [
            (
                pl.ds(agent * local_steps + group * group_steps, group_steps),
                pl.ds(group * group_rows + agent * group_steps, group_steps),
            )
            for agent in range(agents)
        ]

    def to_column(row):
        return jnp.transpose(jnp.broadcast_to(row, (128, row.shape[1])))[:, :1]

    for group in range(groups):
        for source, target in row_spans(group):
            rows = rows_ref[source, :].astype(F32)
            normed_ref[target, :] = (rows * inv_rms(rows) * gain_ref[...]).astype(BF16)
            column[target, :] = jnp.broadcast_to(
                jnp.sum(rows * value_ref[...], axis=-1, keepdims=True), (rows.shape[0], 128)
            )
    normed_out = pltpu.make_async_copy(
        normed_ref, pack_ref.at[pl.ds(0, total_rows), :], out_sems.at[0]
    )
    normed_out.start()
    for copy in copies:
        copy.wait()

    u_parts = jnp.transpose(w_all[:, pl.ds(block_width - 128, 128)].astype(F32))
    u_high, u_low = u_parts[0:1], u_parts[1:2]
    u_ref[...] = u_high + u_low
    part_at = lax.broadcasted_iota(jnp.int32, (2 * HEADS, width), 0)
    head_at = lax.broadcasted_iota(jnp.int32, (2 * HEADS, width), 1) // size
    by_head = jnp.where(
        head_at == part_at % HEADS, jnp.where(part_at < HEADS, u_high, u_low), 0.0
    ).astype(BF16)
    both = dot_nt(by_head[:, :middle], w_v[0][...]) + dot_nt(by_head[:, middle:], w_v[1][...])
    folded = both[:HEADS] + both[HEADS:]
    folded_high = folded.astype(BF16)
    folded_parts = jnp.concatenate(
        [folded_high.astype(F32), folded - folded_high.astype(F32)], axis=0
    ).astype(BF16)
    both = dot_nt(folded_parts, normed_ref[...])
    folded_rows = both[:HEADS] + both[HEADS:]
    for at in range(0, width, TILE):
        qk[:, pl.ds(at, TILE)] = dot_nn(normed_ref[...], w_q[:, pl.ds(at, TILE)]).astype(BF16)
    for at in range(0, width, TILE):
        qk[:, pl.ds(width + at, TILE)] = dot_nn(
            normed_ref[...], w_k[:, pl.ds(at, TILE)]
        ).astype(BF16)

    row_at = lax.broadcasted_iota(jnp.int32, (group_rows, group_rows), 0)
    col_at = lax.broadcasted_iota(jnp.int32, (group_rows, group_rows), 1)
    same_step = row_at % group_steps == col_at % group_steps
    pulls = []
    for group in range(groups):
        group_span = pl.ds(group * group_rows, group_rows)
        alive = alive_ref[group]
        allowed = same_step & ((alive > 0.5) | (row_at == col_at))
        bias = jnp.where(allowed, 0.0, -1e30)
        predicted = column[group_span, :1]
        for head in range(HEADS):
            queries = qk[group_span, pl.ds(head * size, size)]
            keys = qk[group_span, pl.ds(width + head * size, size)]
            scores = dot_nt(queries, keys) * scale + bias
            weights = jnp.exp(scores - jnp.max(scores, axis=-1, keepdims=True))
            probs = weights * (1.0 / jnp.sum(weights, axis=-1, keepdims=True))
            weighted = probs * folded_rows[
                head : head + 1, group * group_rows : (group + 1) * group_rows
            ]
            pooled = jnp.sum(weighted, axis=-1, keepdims=True)
            predicted = predicted + pooled
            probs_all[group * HEADS + head] = probs
            slopes[group * HEADS + head] = (weighted - probs * pooled) * scale
        error = 32.0 * to_column(alive) * (predicted - to_column(target_ref[group]))
        predicted_ref[group] = jnp.transpose(jnp.broadcast_to(predicted, (group_rows, 128)))[:8]
        column[group_span, :] = jnp.broadcast_to(error, (group_rows, 128))
        pull_rows = []
        for head in range(HEADS):
            query_span = pl.ds(head * size, size)
            key_span = pl.ds(width + head * size, size)
            grad_scores = (slopes[group * HEADS + head] * error).astype(BF16)
            grad_qk[group_span, query_span] = dot_nn(
                grad_scores, qk[group_span, key_span]
            ).astype(BF16)
            grad_qk[group_span, key_span] = dot_tn(
                grad_scores, qk[group_span, query_span]
            ).astype(BF16)
            pull_rows.append(
                jnp.sum(probs_all[group * HEADS + head] * error, axis=0, keepdims=True)
            )
        pulls.append(jnp.concatenate(pull_rows, axis=0))
    grad_outs = [
        pltpu.make_async_copy(
            grad_qk.at[:, column_span(core * width, width)], keep_ref, out_sems.at[1]
        ),
        pltpu.make_async_copy(
            grad_qk.at[:, column_span(other * width, width)],
            pack_ref.at[pl.ds(total_rows, total_rows), :],
            out_sems.at[2],
        ),
    ]
    for out in grad_outs:
        out.start()
    pull = jnp.concatenate(pulls, axis=1) if groups > 1 else pulls[0]
    pull = pull.astype(BF16)
    twice = jnp.concatenate([pull, pull], axis=0)
    for at in range(0, width, TILE):
        span = pl.ds(at, TILE)
        grad_normed[:, span] = (
            dot_nt(grad_qk[:, pl.ds(0, width)], w_q[span, :])
            + dot_nt(grad_qk[:, pl.ds(width, width)], w_k[span, :])
            + dot_tn(twice, folded_parts[:, at : at + TILE])
        )
    for group in range(groups):
        for source, target in row_spans(group):
            rows = rows_ref[source, :].astype(F32)
            pulled = norm_pull(rows, gain_ref[...], grad_normed[target, :])
            top = column[target, :1] * value_ref[...]
            grad_ref[source, :] = (top + pulled).astype(BF16)

    folded_grad = dot_nn(pull, normed_ref[...])
    folded_grad_low = folded_grad.astype(BF16)
    pooled = jnp.concatenate(
        [dot_nn(folded_grad_low, w_v[0][...]), dot_nn(folded_grad_low, w_v[1][...])], axis=1
    )
    pooled = jnp.sum(
        jnp.where(head_at[:HEADS] == part_at[:HEADS], pooled, 0.0), axis=0, keepdims=True
    )
    extra = jnp.concatenate(
        [folded_grad, pooled, jnp.zeros((127 - HEADS, width), F32)], axis=0
    )
    extra_ref[...] = jnp.transpose(extra).astype(BF16)
    for out in [normed_out] + grad_outs:
        out.wait()


def weight_grad_kernel(hops, env_ref, tm_ref, pack_ref, keep_ref, moved_ref, extra_ref, *rest):
    outs, (total, sems) = rest[:-2], rest[-2:]
    half, width = keep_ref.shape
    depth = width // len(outs)
    own, other = pl.ds(0, half), pl.ds(half, half)
    total[:, pl.ds(width, 128)] = extra_ref[...]
    for rows in spans(width, TILE):
        for columns in spans(width, TILE):
            total[rows, columns] = (
                dot_tn(pack_ref[own, rows], keep_ref[:, columns])
                + dot_tn(moved_ref[own, rows], moved_ref[other, columns])
            ).astype(BF16)
    copies = [
        pltpu.make_async_copy(
            total.at[
                pl.ds(
                    pl.multiple_of(place_of(env_ref, tm_ref, len(outs), hop) * depth, depth), depth
                ),
                :,
            ],
            out,
            sems.at[at],
        )
        for at, (hop, out) in enumerate(zip(hops, outs))
    ]
    for copy in copies:
        copy.start()
    for copy in copies:
        copy.wait()


def pack_block_kernel(env_ref, qk_ref, v_ref, w_out_ref, value_ref, out_ref):
    width, middle = qk_ref.shape[1], v_ref.shape[1]
    out_ref[:, pl.ds(0, width)] = qk_ref[...]
    out_ref[:, pl.ds(width, middle)] = v_ref[...]
    u = jnp.sum(w_out_ref[...].astype(F32) * value_ref[...], axis=-1, keepdims=True)
    high = u.astype(BF16).astype(F32)
    lane = lax.broadcasted_iota(jnp.int32, (qk_ref.shape[0], 128), 1)
    parts = jnp.where(lane == 0, high, jnp.where(lane == 1, u - high, 0.0))
    out_ref[:, pl.ds(width + middle, 128)] = parts.astype(BF16)


def finish_kernel(env_ref, own_ref, other_ref, u_ref, value_ref, qkv_ref, out_ref):
    width = u_ref.shape[1]
    size = width // HEADS
    own, other = own_ref[:, pl.ds(0, width)], other_ref[:, pl.ds(0, width)]
    core = core_of(env_ref)
    qkv_ref[:, pl.ds(pl.multiple_of(core * width, width), width)] = own.astype(F32)
    qkv_ref[:, pl.ds(pl.multiple_of((1 - core) * width, width), width)] = other.astype(F32)
    extra = own_ref[:, pl.ds(width, 128)].astype(F32) + other_ref[:, pl.ds(width, 128)].astype(F32)
    for head in range(HEADS):
        qkv_ref[:, pl.ds(2 * width + head * size, size)] = (
            extra[:, head : head + 1] * u_ref[:, pl.ds(head * size, size)]
        )
    out_ref[...] = extra[:, HEADS : HEADS + 1] * value_ref[...]


def any_spec():
    return pl.BlockSpec(memory_space=pl.ANY)


def hbm_spec():
    return pl.BlockSpec(memory_space=pltpu.HBM)


def vmem_spec():
    return pl.BlockSpec(memory_space=pltpu.VMEM)


def smem_spec():
    return pl.BlockSpec(memory_space=pltpu.SMEM)


def params(mebibytes=60):
    return pltpu.CompilerParams(vmem_limit_bytes=mebibytes * 1024 * 1024)


def cost(microseconds):
    return pl.CostEstimate(
        flops=int(microseconds * 1e9), bytes_accessed=int(microseconds * 2e6), transcendentals=0
    )


def ring_order(count):
    return list(range(0, count, 2)) + list(range(count - 1, 0, -2))


def per_device(
    env_count, tm_count,
    hidden, done_step, alive, targets, gain_t, w_qkv_t, w_out_t, gain_a, w_qkv_a, w_out_a, w_value,
):
    length, width = hidden.shape[2:]
    agents, local_steps = alive.shape[1:]
    depth = w_qkv_a.shape[0]
    env_index = lax.axis_index("env").astype(jnp.int32)[None]
    tm_index = lax.axis_index("tm").astype(jnp.int32)[None]
    order = ring_order(tm_count)
    spot = [order.index(at) for at in range(tm_count)]

    ways = [1 if at in (0, 3) else -1 for at in range(env_count)]

    def ring(block, along=1):
        pairs = [
            (env * tm_count + at, env * tm_count + order[(spot[at] + along * ways[env]) % tm_count])
            for env in range(env_count)
            for at in range(tm_count)
        ]
        return lax.ppermute(block, ("env", "tm"), pairs)

    def ring_other_chip(block):
        pairs = [
            (env * tm_count + at, (env ^ 2) * tm_count + order[(spot[at] + ways[env]) % tm_count])
            for env in range(env_count)
            for at in range(tm_count)
        ]
        return lax.ppermute(block, ("env", "tm"), pairs)

    def swap_core(block):
        return lax.ppermute(block, "env", [(at, at ^ 1) for at in range(env_count)])

    def swap_chip(block):
        return lax.ppermute(block, "env", [(at, at ^ 2) for at in range(env_count)])

    far = tm_count // 2
    near = tm_count - 1 - far

    block_width = width + width // 2 + 128
    own_block = pl.pallas_call(
        pack_block_kernel,
        name="pack_block",
        out_shape=jax.ShapeDtypeStruct((depth, block_width), BF16),
        grid_spec=pltpu.PrefetchScalarGridSpec(
            num_scalar_prefetch=1,
            grid=(1,),
            in_specs=[
                pl.BlockSpec((depth, width), lambda at, env: (0, core_of(env))),
                pl.BlockSpec((depth, width // 2), lambda at, env: (0, 4 + core_of(env))),
                pl.BlockSpec((depth, width), lambda at, env: (0, 0)),
                pl.BlockSpec((1, width), lambda at, env: (0, 0)),
            ],
            out_specs=pl.BlockSpec((depth, block_width), lambda at, env: (0, 0)),
        ),
        compiler_params=params(),
        cost_estimate=cost(2),
    )(env_index, w_qkv_a, w_qkv_a, w_out_a, w_value[None])
    first_block = ring(own_block)

    rows = hidden[0, 0]
    h1, qkv, probs = pl.pallas_call(
        temporal_forward,
        name="temporal_forward",
        out_shape=(
            jax.ShapeDtypeStruct((length, width), BF16),
            jax.ShapeDtypeStruct((length, 3 * width), BF16),
            jax.ShapeDtypeStruct((HEADS, length, length), BF16),
        ),
        in_specs=[smem_spec()] + [vmem_spec()] * 2 + [hbm_spec()] * 2,
        out_specs=[vmem_spec()] + [hbm_spec()] * 2,
        scratch_shapes=[
            pltpu.VMEM((width, 3 * width), BF16),
            pltpu.VMEM((width, width), BF16),
            pltpu.VMEM((length, 3 * width), BF16),
            pltpu.VMEM((HEADS, length, length), BF16),
            pltpu.VMEM((length, width), BF16),
            pltpu.SemaphoreType.DMA((7,)),
            pltpu.SemaphoreType.DMA((HEADS + 1,)),
        ],
        compiler_params=params(),
        cost_estimate=cost(8),
    )(done_step[0], rows, gain_t[None], w_qkv_t, w_out_t)
    h1, first_block = lax.optimization_barrier((h1, first_block))
    lifted = lax.all_to_all(h1, "tm", split_axis=0, concat_axis=0, tiled=True)

    ringed, crossed = [first_block], []
    for hop in range(1, far):
        if len(crossed) > 0:
            ringed[-1], crossed[-1] = lax.optimization_barrier((ringed[-1], crossed[-1]))
        if hop <= near:
            crossed.append(swap_chip(ringed[-1]))
        ringed.append(ring(ringed[-1]))
    crossed += [swap_chip(block) for block in ringed[len(crossed) : near]]
    own_blocks = ringed + crossed
    gated = far + near // 2
    lifted, own_blocks[gated] = lax.optimization_barrier((lifted, own_blocks[gated]))
    other_blocks = [swap_core(block) for block in own_blocks]

    group_steps = 16 if local_steps % 16 == 0 else local_steps
    groups = local_steps // group_steps
    group_rows = agents * group_steps

    def grouped(block):
        block = block.reshape(agents, groups, group_steps)
        return jnp.swapaxes(block, 0, 1).reshape(groups, 1, group_rows)

    total_rows = agents * local_steps
    grad_lifted, pack, keep, extra, u, predicted = pl.pallas_call(
        functools.partial(agent_kernel, tm_count - 1, group_steps),
        name="agent_block",
        out_shape=(
            jax.ShapeDtypeStruct((total_rows, width), BF16),
            jax.ShapeDtypeStruct((2 * total_rows, width), BF16),
            jax.ShapeDtypeStruct((total_rows, width), BF16),
            jax.ShapeDtypeStruct((width, 128), BF16),
            jax.ShapeDtypeStruct((1, width), F32),
            jax.ShapeDtypeStruct((groups, 8, group_rows), F32),
        ),
        in_specs=[smem_spec()] * 2 + [vmem_spec()] * 5 + [hbm_spec()] * (2 * tm_count),
        out_specs=[vmem_spec()] + [hbm_spec()] * 2 + [vmem_spec()] * 3,
        scratch_shapes=[
            pltpu.VMEM((width, 2 * block_width), BF16),
            pltpu.VMEM((total_rows, 2 * width), BF16),
            pltpu.VMEM((total_rows, 2 * width), BF16),
            pltpu.VMEM((groups * HEADS, group_rows, group_rows), F32),
            pltpu.VMEM((groups * HEADS, group_rows, group_rows), F32),
            pltpu.VMEM((total_rows, 128), F32),
            pltpu.VMEM((total_rows, width), F32),
            pltpu.VMEM((total_rows, width), BF16),
            pltpu.SemaphoreType.DMA((2 * tm_count + 2,)),
            pltpu.SemaphoreType.DMA((3,)),
        ],
        compiler_params=params(),
        cost_estimate=cost(11),
    )(
        env_index, tm_index, lifted, grouped(alive[0].astype(F32)), grouped(targets[0]), gain_a[None],
        w_value[None], w_qkv_a, own_block, *own_blocks, *other_blocks,
    )
    values = predicted[:, 0].reshape(groups, agents, group_steps)
    values = jnp.swapaxes(values, 0, 1).reshape(1, agents, local_steps)

    returned = lax.all_to_all(grad_lifted, "tm", split_axis=0, concat_axis=0, tiled=True)

    moved = swap_core(pack)
    hops = list(range(far + 1)) + [-hop for hop in range(1, near + 1)]
    terms = pl.pallas_call(
        functools.partial(weight_grad_kernel, hops),
        name="weight_grad",
        out_shape=[jax.ShapeDtypeStruct((depth, width + 128), BF16)] * tm_count,
        in_specs=[smem_spec()] * 2 + [vmem_spec()] * 4,
        out_specs=[any_spec()] * tm_count,
        scratch_shapes=[
            pltpu.VMEM((width, width + 128), BF16),
            pltpu.SemaphoreType.DMA((tm_count,)),
        ],
        compiler_params=params(20),
        cost_estimate=cost(4),
    )(env_index, tm_index, pack, keep, moved, extra)
    def mix_grad(first_head):
        heads, part = HEADS // 2, width // 2
        return pl.pallas_call(
            functools.partial(mix_grad_kernel, first_head),
            name="temporal_mix_grad",
            out_shape=jax.ShapeDtypeStruct((length, 3 * part), BF16),
            in_specs=[hbm_spec()] * 4,
            out_specs=vmem_spec(),
            scratch_shapes=[
                pltpu.VMEM((length, width), BF16),
                pltpu.VMEM((part, width), BF16),
                pltpu.VMEM((length, 3 * part), BF16),
                pltpu.VMEM((heads, length, length), BF16),
                pltpu.VMEM((length, part), BF16),
                pltpu.SemaphoreType.DMA((part // TILE + 5,)),
            ],
            compiler_params=params(),
            cost_estimate=cost(4),
        )(returned, w_out_t, qkv, probs)

    term = dict(zip(hops, terms))
    travelling = ring(term[far])
    chip_terms = {hop: swap_chip(term[-hop]) for hop in range(near, 1, -1)}
    arriving = ring(term[-1], -1)
    for hop in range(far - 1, 0, -1):
        if hop == far - 1:
            travelling, returned, arriving = lax.optimization_barrier(
                (travelling, returned, arriving)
            )
            near_sum = (arriving.astype(F32) + term[0].astype(F32)).astype(BF16)
            far_sum = swap_chip(near_sum)
        if hop == max(far - 2, 1):
            travelling, low_grads = lax.optimization_barrier((travelling, mix_grad(0)))
        if hop == max(far - 3, 1):
            travelling, high_grads, far_sum = lax.optimization_barrier(
                (travelling, mix_grad(HEADS // 2), far_sum)
            )
        total = travelling.astype(F32) + term[hop].astype(F32)
        if hop in chip_terms:
            total = total + chip_terms[hop].astype(F32)
        total = total.astype(BF16)
        if hop == 1:
            crossing = ring_other_chip(total)
        travelling = ring(total)
    input_grad = pl.pallas_call(
        norm_grad_kernel,
        name="temporal_norm_grad",
        out_shape=jax.ShapeDtypeStruct((length, width), BF16),
        in_specs=[vmem_spec()] + [hbm_spec()] * 5,
        out_specs=vmem_spec(),
        scratch_shapes=[
            pltpu.VMEM((length, width), BF16),
            pltpu.VMEM((length, width), BF16),
            pltpu.VMEM((length, 3 * width // 2), BF16),
            pltpu.VMEM((length, 3 * width // 2), BF16),
            pltpu.VMEM((width, 3 * width), BF16),
            pltpu.VMEM((length, width), F32),
            pltpu.SemaphoreType.DMA((width // TILE + 4,)),
        ],
        compiler_params=params(),
        cost_estimate=cost(6),
    )(gain_t[None], returned, rows, low_grads, high_grads, w_qkv_t)
    reduced = travelling.astype(F32) + crossing.astype(F32)
    reduced = (reduced + near_sum.astype(F32) + far_sum.astype(F32)).astype(BF16)
    reduced, values, input_grad = lax.optimization_barrier((reduced, values, input_grad))
    other = swap_core(reduced)
    qkv_grad, out_grad = pl.pallas_call(
        finish_kernel,
        name="finish",
        out_shape=(
            jax.ShapeDtypeStruct((depth, 3 * width), F32),
            jax.ShapeDtypeStruct((depth, width), F32),
        ),
        in_specs=[smem_spec()] + [vmem_spec()] * 4,
        out_specs=[vmem_spec()] * 2,
        compiler_params=params(14),
        cost_estimate=cost(2),
    )(env_index, reduced, other, u, w_value[None])
    return values, input_grad[None, None], qkv_grad, out_grad


def solution(mesh):
    in_specs = (
        P("env", "tm", None, None),
        P("env", "tm"),
        P("env", None, "tm"),
        P("env", None, "tm"),
        P(),
        P(),
        P(),
        P(),
        P("tm", None),
        P("tm", None),
        P(),
    )
    out_specs = (P("env", None, "tm"), P("env", "tm", None, None), P("tm", None), P("tm", None))
    body = functools.partial(per_device, mesh.shape["env"], mesh.shape["tm"])
    return jax.shard_map(
        body, mesh=mesh, in_specs=in_specs, out_specs=out_specs, check_vma=False
    )
```
